128 devices in a mesh: gy: 8 (over z_hi, y), gx: 16 (over x, z_lo, core).
Axes of the slice: x: 4, y: 4, z: 4 (z_hi: 2, z_lo: 2; z = z_hi * 2 + z_lo), core: 2. Of those that a mesh axis runs over, the one named last changes fastest.
Arguments:
- obj: float32 [2, 2048, 4096], P(None, 'gy', 'gx'), may hold values from -5 to 5
- probe: float32 [2, 256, 256], replicated, may hold values from -6 to 6
- positions: int32 [8, 16, 8, 2], P('gy', 'gx'), may hold values from -128 to 3967, as said below
- amps: bfloat16 [8, 16, 8, 256, 256], P('gy', 'gx'), may hold values from 0 to 2
Outputs:
- obj_new: float32 [2, 2048, 4096], P(None, 'gy', 'gx')
- probe_new: float32 [2, 256, 256], replicated
The draws below stay inside these ranges and needn't reach their ends.
Inputs may be any that keep to these rules, and one draw needn't show every extreme that they name: `positions`: for the entry at [ty, tx, k], both coordinates plus 128 lie in the tile, that is row within [ty * 256, (ty + 1) * 256) and column within [tx * 256, (tx + 1) * 256).
All inputs are finite; a program needn't handle non-finite values.
Results may differ from the reference program's by a relative error of at most 0.0003.
Values sent between devices are 32-bit elements; how exact they have to be, the bound alone decides.
A program may use at most 128 MiB of HBM per device.

```python
import jax
import jax.numpy as jnp
from jax import lax

PATCH = 256
HALF = 128
TILE = 256
POS_DEV = 8
ITERS = 2
TILES_Y = 8
TILES_X = 16
NY = 2048
NX = 4096


def draw_positions(key, part):
    key = jax.random.fold_in(key, 7)
    offsets = jax.random.randint(key, (TILES_Y, TILES_X, POS_DEV, 2), 0, TILE)
    slot = jnp.arange(POS_DEV)[None, None, :, None]
    which = jnp.arange(2)[None, None, None, :]
    offsets = jnp.where((slot == 0) & (which == 0), 0, offsets)
    offsets = jnp.where((slot == 1) & (which == 1), TILE - 1, offsets)
    rows = jnp.arange(TILES_Y)[:, None, None, None] * TILE
    cols = jnp.arange(TILES_X)[None, :, None, None] * TILE
    anchor = jnp.where(which == 0, rows, cols)
    return (anchor + offsets - HALF).astype(jnp.int32)


def shard_levels(own_key, dims, cuts, smallest, top_value):
    level, own = 1.0, jax.random.fold_in(own_key, 6)
    for dim, parts in cuts:
        steps = jnp.exp(jax.random.uniform(jax.random.fold_in(own, dim), (parts,), jnp.float32, smallest / len(cuts), top_value / len(cuts)))
        level = level * jnp.repeat(steps, dims[dim] // parts).reshape([-1 if axis == dim else 1 for axis in range(len(dims))])
    return level


def noise(key, dims, width, bound, shards=(), kind=jnp.bfloat16):
    loudness = shard_levels(key, dims, shards, -0.22, 0.18) if shards else 1.0
    values = jax.random.normal(key, dims, jnp.float32) * width * loudness
    return jnp.minimum(jnp.maximum(values, -bound), bound).astype(kind)


def setup_inputs(seed: int = 0) -> dict:
    seeds = jax.random.split(jax.random.key(seed), 5)
    return {
        "obj": noise(seeds[0], (2, NY, NX), 0.7, 5.0, ((1, 8), (2, 16)), jnp.float32),
        "probe": noise(seeds[1], (2, PATCH, PATCH), 1.0, 6.0, (), jnp.float32),
        "positions": draw_positions(jax.random.fold_in(seeds[4], 71), 0),
        "amps": jnp.clip(2.0 * jax.random.uniform(seeds[3], (TILES_Y, TILES_X, POS_DEV, PATCH, PATCH), jnp.float32) ** shard_levels(seeds[3], (TILES_Y, TILES_X, POS_DEV, PATCH, PATCH), ((0, 8), (1, 16)), -0.2, 0.2), 0.0, 2.0).astype(jnp.bfloat16),
    }


def reference(obj, probe, positions, amps):
    objc = lax.complex(obj[0], obj[1])
    probec = lax.complex(probe[0], probe[1])
    spots = positions.reshape(-1, 2).astype(jnp.int32)
    measured = amps.reshape(-1, PATCH, PATCH).astype(jnp.float32)
    for step in range(ITERS):
        padded = jnp.pad(objc, HALF)

        def visit(carry, item):
            grad_obj, grad_probe, weight = carry
            corner, target = item
            row = (corner[0] + HALF).astype(jnp.int32)
            col = (corner[1] + HALF).astype(jnp.int32)
            patch = lax.dynamic_slice(padded, (row, col), (PATCH, PATCH))
            far = jnp.fft.fft2(probec * patch, norm="ortho")
            magnitude = jnp.maximum(jnp.abs(far), 0.5)
            chi = jnp.fft.ifft2(far * (target / magnitude - 1.0), norm="ortho")
            current = lax.dynamic_slice(grad_obj, (row, col), (PATCH, PATCH))
            grad_obj = lax.dynamic_update_slice(grad_obj, current + jnp.conj(probec) * chi, (row, col))
            grad_probe = grad_probe + jnp.conj(patch) * chi
            weight = weight + jnp.real(patch) ** 2 + jnp.imag(patch) ** 2
            return (grad_obj, grad_probe, weight), None

        start = (jnp.zeros_like(padded), jnp.zeros_like(probec), jnp.zeros(probe.shape[1:], probe.dtype))
        (grad_obj, grad_probe, weight), unused = lax.scan(visit, start, (spots, measured))
        grad_obj = grad_obj[HALF:-HALF, HALF:-HALF]
        peak = jnp.max(jnp.real(probec) ** 2 + jnp.imag(probec) ** 2)
        objc = objc + grad_obj / peak
        probec = probec + grad_probe / (0.9 * weight + 0.1 * jnp.max(weight))
    return (jnp.stack([jnp.real(objc), jnp.imag(objc)]), jnp.stack([jnp.real(probec), jnp.imag(probec)]))
```

```python
import functools

import jax
import jax.numpy as jnp
import ml_dtypes
import numpy as np
from jax import lax
from jax.experimental import pallas as pl
from jax.experimental.pallas import tpu as pltpu
from jax.sharding import PartitionSpec as P

MESH = pl.DeviceIdType.MESH
F32 = jnp.float32
BF16 = jnp.bfloat16
VMEM = pl.BlockSpec(memory_space=pltpu.VMEM)
SMEM = pl.BlockSpec(memory_space=pltpu.SMEM)
VMEM_LIMIT = 60 * 1024 * 1024

DIRS = [(-1, 0), (1, 0), (0, -1), (0, 1), (-1, -1), (-1, 1), (1, -1), (1, 1)]


def tables():
    n = np.arange(128)[:, None]
    out = []
    for parity in range(2):
        turns = (n * (2 * np.arange(128)[None, :] + parity)) % 256
        angle = -2.0 * np.pi * turns / 256.0
        re, im = np.cos(angle) / 16.0, np.sin(angle) / 16.0
        m = np.block([[re, im], [-im, re]]).astype(np.float32)
        hi = m.astype(ml_dtypes.bfloat16)
        lo = (m - hi.astype(np.float32)).astype(ml_dtypes.bfloat16)
        out.append(np.stack([hi, lo]))
    right = np.stack(out)
    return right, np.ascontiguousarray(np.swapaxes(right, 2, 3))


def sorting():
    m = np.zeros((256, 256), np.float32)
    m[np.arange(256), np.concatenate([np.arange(0, 256, 2), np.arange(1, 256, 2)])] = 1.0
    return np.stack([m, m.T]).astype(ml_dtypes.bfloat16)


def neighbor(dy, dx):
    y = lax.axis_index("gy") + dy
    x = lax.axis_index("gx") + dx
    ny, nx = lax.axis_size("gy"), lax.axis_size("gx")
    ok = (y >= 0) & (y < ny) & (x >= 0) & (x < nx)
    return ok, (jnp.clip(y, 0, ny - 1), jnp.clip(x, 0, nx - 1))


def halo_region(dy, dx):
    rows = {-1: slice(0, 128), 0: slice(128, 384), 1: slice(384, 512)}[dy]
    cols = {-1: slice(0, 1), 0: slice(1, 3), 1: slice(3, 4)}[dx]
    return cols, rows


def edge_region(dy, dx):
    rows = {-1: slice(128, 256), 0: slice(128, 384), 1: slice(256, 384)}[dy]
    cols = {-1: slice(1, 2), 0: slice(1, 3), 1: slice(2, 3)}[dx]
    return cols, rows


def greet_sides():
    barrier = pltpu.get_barrier_semaphore()
    count = jnp.int32(0)
    for d in DIRS:
        ok, device = neighbor(*d)

        @pl.when(ok)
        def _(device=device):
            pl.semaphore_signal(barrier, inc=1, device_id=device, device_id_type=MESH)

        count = count + ok.astype(jnp.int32)
    return barrier, count


def side_copies(source, target, outward, send, recv):
    out = []
    for i, (dy, dx) in enumerate(DIRS):
        ok, device = neighbor(dy, dx)
        cols, rows = edge_region(dy, dx) if outward else halo_region(dy, dx)
        tcols, trows = halo_region(-dy, -dx) if outward else (cols, rows)
        out.append(
            (
                ok,
                neighbor(-dy, -dx)[0],
                pltpu.make_async_remote_copy(
                    source.at[:, cols, rows, :],
                    target.at[:, tcols, trows, :],
                    send.at[i],
                    recv.at[i],
                    device_id=device,
                    device_id_type=MESH,
                ),
            )
        )
    return out


def start_sides(copies):
    for ok, _, copy in copies:
        pl.when(ok)(copy.start)


def wait_sides(copies):
    for ok, arrives, copy in copies:
        pl.when(ok)(copy.wait_send)
        pl.when(arrives)(copy.wait_recv)


def blank_outside(ext):
    for dy, dx in DIRS:
        cols, rows = halo_region(dy, dx)

        @pl.when(jnp.logical_not(neighbor(dy, dx)[0]))
        def _(cols=cols, rows=rows):
            ext[:, cols, rows, :] = jnp.zeros((2, cols.stop - cols.start, rows.stop - rows.start, 128), F32)


def halo_kernel(obj, amps, sort, ext, amps_out, send, recv):
    blank_outside(ext)
    barrier, count = greet_sides()
    for b in range(2):
        ext[:, 1 + b, 128:384, :] = obj[:, :, 128 * b : 128 * b + 128]
    pl.semaphore_wait(barrier, count)
    copies = side_copies(ext, ext, True, send, recv)
    start_sides(copies)

    def arrange(k, carry):
        half = jnp.dot(sort[0], amps[k], preferred_element_type=F32).astype(BF16)
        amps_out[k] = jnp.dot(half, sort[1], preferred_element_type=F32).astype(BF16)
        return carry

    lax.fori_loop(0, amps.shape[0], arrange, jnp.int32(0))
    wait_sides(copies)


def split(x):
    hi = x.astype(BF16)
    return hi, (x - hi.astype(F32)).astype(BF16)


def right_dot(hi, lo, m):
    return jnp.dot(
        jnp.concatenate([hi, lo, hi], axis=1),
        jnp.concatenate([m[0], m[0], m[1]], axis=0),
        preferred_element_type=F32,
    )


def left_dot(m, hi, lo):
    return jnp.dot(
        jnp.concatenate([m[0], m[0], m[1]], axis=1),
        jnp.concatenate([hi, lo, hi], axis=0),
        preferred_element_type=F32,
    )


def compute_kernel(local, ext, probe, amps, right, left, grad, total, cut, lhs_hi, lhs_lo):
    grad[...] = jnp.zeros_like(grad)
    total[...] = jnp.zeros_like(total)
    lane = lax.broadcasted_iota(jnp.int32, (1, 128), 1)

    def visit(k, carry):
        r = local[k, 0]
        c = local[k, 1]
        first = lax.div(c, 128)
        c = lax.rem(c, 128)
        back = lax.rem(128 - c, 128)
        keep = lane < 128 - c
        late = lane >= c
        for i in range(0, 256, 64):
            rows = slice(i, i + 64)
            part = []
            for p in range(2):
                t = [pltpu.roll(ext[p, first + b, pl.ds(r + i, 64), :], back, 1) for b in range(3)]
                h = [jnp.where(keep, t[0], t[1]), jnp.where(keep, t[1], t[2])]
                for b in range(2):
                    cut[p, b, rows, :] = h[b]
                part.append(h)
            wave = []
            for b in range(2):
                ore, oim = part[0][b], part[1][b]
                pre, pim = probe[0, b, rows, :], probe[1, b, rows, :]
                total[2, b, rows, :] += ore * ore + oim * oim
                wave.append((pre * ore - pim * oim, pre * oim + pim * ore))
            for q in range(2):
                for p in range(2):
                    x = wave[0][p] + wave[1][p] if q == 0 else wave[0][p] - wave[1][p]
                    hi, lo = split(x)
                    lhs_hi[q, rows, 128 * p : 128 * p + 128] = hi
                    lhs_lo[q, rows, 128 * p : 128 * p + 128] = lo
        y = [right_dot(lhs_hi[q], lhs_lo[q], right[q]) for q in range(2)]
        half = []
        for s in range(2):
            pieces = []
            for p in range(2):
                lanes = slice(128 * p, 128 * p + 128)
                top = jnp.concatenate([y[0][:128, lanes], y[1][:128, lanes]], axis=1)
                low = jnp.concatenate([y[0][128:, lanes], y[1][128:, lanes]], axis=1)
                pieces.append(top + low if s == 0 else top - low)
            hi, lo = split(jnp.concatenate(pieces, axis=0))
            far = left_dot(left[s], hi, lo)
            re, im = far[:128], far[128:]
            factor = amps[k, 128 * s : 128 * s + 128, :].astype(F32) * lax.rsqrt(jnp.maximum(re * re + im * im, 0.25)) - 1.0
            hi, lo = split(jnp.concatenate([re * factor, im * factor], axis=0))
            half.append(left_dot(right[s], hi, lo))
        top, low = half[0] + half[1], half[0] - half[1]
        chi = []
        for q in range(2):
            lanes = slice(128 * q, 128 * q + 128)
            x = jnp.concatenate(
                [
                    jnp.concatenate([top[:128, lanes], top[128:, lanes]], axis=1),
                    jnp.concatenate([low[:128, lanes], low[128:, lanes]], axis=1),
                ],
                axis=0,
            )
            hi, lo = split(x)
            chi.append(right_dot(hi, lo, left[q]))
        for i in range(0, 256, 64):
            rows = slice(i, i + 64)
            g = [[], []]
            for b in range(2):
                x = chi[0][rows] + chi[1][rows] if b == 0 else chi[0][rows] - chi[1][rows]
                cre, cim = x[:, :128], x[:, 128:]
                pre, pim = probe[0, b, rows, :], probe[1, b, rows, :]
                ore, oim = cut[0, b, rows, :], cut[1, b, rows, :]
                total[0, b, rows, :] += ore * cre + oim * cim
                total[1, b, rows, :] += ore * cim - oim * cre
                g[0].append(pltpu.roll(pre * cre + pim * cim, c, 1))
                g[1].append(pltpu.roll(pre * cim - pim * cre, c, 1))
            for p in range(2):
                grad[p, first, pl.ds(r + i, 64), :] += jnp.where(late, g[p][0], 0.0)
                grad[p, first + 1, pl.ds(r + i, 64), :] += jnp.where(late, g[p][1], g[p][0])
                grad[p, first + 2, pl.ds(r + i, 64), :] += jnp.where(late, 0.0, g[p][1])
        return carry

    lax.fori_loop(0, amps.shape[0], visit, jnp.int32(0))


def group_ids():
    gy, gx = lax.axis_index("gy"), lax.axis_index("gx")
    return lax.rem(gx, 2), lax.rem(gy, 4), lax.div(gy, 4) * 8 + lax.div(gx, 2)


def sibling():
    gy, gx = lax.axis_index("gy"), lax.axis_index("gx")
    return gy, gx + 1 - 2 * lax.rem(gx, 2)


def along_y(d):
    gy, gx = lax.axis_index("gy"), lax.axis_index("gx")
    y = lax.rem(gy, 4)
    return gy - y + lax.rem(y + d, 4), gx


def member(j):
    gy, gx = lax.axis_index("gy"), lax.axis_index("gx")
    return lax.div(j, 8) * 4 + lax.rem(gy, 4), lax.rem(j, 8) * 2 + lax.rem(gx, 2)


class Sum:
    def __init__(self, total, full, acc0, acc1, acc2, rb0, rb1, rb2, sems):
        self.total, self.full, self.acc0, self.acc1, self.acc2 = total, full, acc0, acc1, acc2
        self.rb0, self.rb1, self.rb2 = rb0, rb1, rb2
        self.sems = sems
        self.core, self.y, self.me = group_ids()
        self.mine = lax.rem(self.me, 8)

    def greet(self, barrier):
        devices = [sibling()] + [along_y(d) for d in (1, 2, 3)] + [member(lax.rem(self.me + d, 16)) for d in range(1, 16)]
        for device in devices:
            pl.semaphore_signal(barrier, inc=1, device_id=device, device_id_type=MESH)
        return len(devices)

    def copy(self, source, target, i, j, device):
        send, recv = self.sems
        return pltpu.make_async_remote_copy(
            source, target, send.at[i], recv.at[j], device_id=device, device_id_type=MESH
        )

    def step0(self):
        theirs = pl.ds(pl.multiple_of((1 - self.core) * 128, 128), 128)
        self.c0 = self.copy(self.total.at[:, theirs, :], self.rb0, 0, 0, sibling())
        self.c0.start()

    def step1(self):
        self.c0.wait_recv()
        own = pl.ds(pl.multiple_of(self.core * 128, 128), 128)
        self.acc0[...] = self.total[:, own, :] + self.rb0[...]
        self.c1 = []
        for d in (1, 2, 3):
            part = pl.ds(pl.multiple_of(lax.rem(self.y + d, 4) * 32, 32), 32)
            c = self.copy(self.acc0.at[:, part, :], self.rb1.at[d - 1], d, d, along_y(d))
            c.start()
            self.c1.append(c)

    def step2(self):
        for c in self.c1:
            c.wait_recv()
        own = pl.ds(pl.multiple_of(self.y * 32, 32), 32)
        x = self.acc0[:, own, :] + self.rb1[0] + self.rb1[1] + self.rb1[2]
        self.acc1[...] = x.reshape(24, 8, 128)
        self.rb2[pl.ds(self.me, 1)] = self.acc1[pl.ds(self.mine * 3, 3)][None]
        self.c2 = []
        for d in range(1, 16):
            to = lax.rem(self.me + d, 16)
            c = self.copy(
                self.acc1.at[pl.ds(lax.rem(to, 8) * 3, 3)], self.rb2.at[self.me], 3 + d, 3 + d, member(to)
            )
            c.start()
            self.c2.append(c)

    def step3(self):
        for c in self.c2:
            c.wait_recv()
        x = self.rb2[0]
        for j in range(1, 16):
            x = x + self.rb2[j]
        self.acc2[...] = x
        place = self.full.at[self.core, self.y, pl.ds(self.mine * 3, 3)]
        self.full[pl.ds(self.core, 1), pl.ds(self.y, 1), pl.ds(self.mine * 3, 3)] = x[None, None]
        self.c3 = []
        for d in range(1, 8):
            to = lax.rem(self.mine + d, 8) + lax.div(self.me, 8) * 8
            c = self.copy(self.acc2, place, 18 + d, 18 + d, member(to))
            c.start()
            self.c3.append(c)

    def step4(self):
        for c in self.c3:
            c.wait_recv()
        self.c4 = []
        for d in (1, 2, 3):
            place = self.full.at[self.core, self.y]
            c = self.copy(place, place, 25 + d, 25 + d, along_y(d))
            c.start()
            self.c4.append(c)

    def step5(self):
        for c in self.c4:
            c.wait_recv()
        place = self.full.at[self.core]
        self.c5 = self.copy(place, place, 29, 29, sibling())
        self.c5.start()

    def finish(self):
        self.c5.wait_recv()
        for c in [self.c0, *self.c1, *self.c2, *self.c3, *self.c4, self.c5]:
            c.wait_send()


SUM_SCRATCH = [
    pltpu.VMEM((2, 4, 24, 8, 128), F32),
    pltpu.VMEM((6, 128, 128), F32),
    pltpu.VMEM((24, 8, 128), F32),
    pltpu.VMEM((3, 8, 128), F32),
    pltpu.VMEM((6, 128, 128), F32),
    pltpu.VMEM((3, 6, 32, 128), F32),
    pltpu.VMEM((16, 3, 8, 128), F32),
    pltpu.SemaphoreType.DMA((30,)),
    pltpu.SemaphoreType.DMA((30,)),
]


def new_probe(probe, full, write):
    weights = [full[h, y, 16:24] for h in range(2) for y in range(4)]
    top = weights[0]
    for w in weights[1:]:
        top = jnp.maximum(top, w)
    floor = 0.1 * jnp.max(top)
    for h in range(2):
        for y in range(4):
            rows = slice(128 * h + 32 * y, 128 * h + 32 * y + 32)
            for b in range(2):
                w = 0.9 * full[h, y, 16 + 4 * b : 20 + 4 * b].reshape(32, 128) + floor
                for p in range(2):
                    g = full[h, y, 8 * p + 4 * b : 8 * p + 4 * b + 4].reshape(32, 128)
                    write(p, b, rows, probe[p, b, rows, :] + g / w)


def step_kernel(last, ext, grad, total, probe, *refs):
    if last:
        obj_out, probe_out, inbox, acc, send, recv, *rest = refs
    else:
        ext_out, probe_out, inbox, acc, send, recv, send2, recv2, *rest = refs
    full, acc0, acc1, acc2, rb0, rb1, rb2, ssem, rsem = rest
    adder = Sum(total, full, acc0, acc1, acc2, rb0, rb1, rb2, (ssem, rsem))
    if not last:
        blank_outside(ext_out)
    barrier, count = greet_sides()
    count = count + adder.greet(barrier)
    pl.semaphore_wait(barrier, count)
    adder.step0()
    copies = side_copies(grad, inbox, False, send, recv)
    start_sides(copies)
    peak = jnp.max(probe[0] * probe[0] + probe[1] * probe[1])
    adder.step1()
    acc[...] = grad[:, 1:3, 128:384, :]
    adder.step2()
    wait_sides(copies)
    for i, (dy, dx) in enumerate(DIRS):
        cols, rows = halo_region(dy, dx)
        tcols, trows = edge_region(-dy, -dx)

        @pl.when(neighbor(-dy, -dx)[0])
        def _(cols=cols, rows=rows, tcols=tcols, trows=trows):
            acc[:, tcols.start - 1 : tcols.stop - 1, trows.start - 128 : trows.stop - 128, :] += inbox[:, cols, rows, :]

    if last:
        for b in range(2):
            obj_out[:, :, 128 * b : 128 * b + 128] = ext[:, 1 + b, 128:384, :] + acc[:, b] / peak
    else:
        ext_out[:, 1:3, 128:384, :] = ext[:, 1:3, 128:384, :] + acc[...] / peak
        copies = side_copies(ext_out, ext_out, True, send2, recv2)
        start_sides(copies)
    adder.step3()
    adder.step4()
    adder.step5()
    adder.finish()

    def write(p, b, rows, x):
        if last:
            probe_out[p, rows, 128 * b : 128 * b + 128] = x
        else:
            probe_out[p, b, rows, :] = x

    new_probe(probe, full, write)
    if not last:
        wait_sides(copies)


EXT = jax.ShapeDtypeStruct((2, 4, 512, 128), F32)
BLOCKS = jax.ShapeDtypeStruct((2, 2, 256, 128), F32)
TILE = jax.ShapeDtypeStruct((2, 256, 256), F32)


def params(collective=None):
    if collective is None:
        return pltpu.CompilerParams(vmem_limit_bytes=VMEM_LIMIT)
    return pltpu.CompilerParams(collective_id=collective, has_side_effects=True, vmem_limit_bytes=VMEM_LIMIT)


def shards(obj, probe, positions, amps):
    count = positions.shape[2]
    anchor = jnp.stack([lax.axis_index("gy") * 256, lax.axis_index("gx") * 256])
    local = positions.reshape(count, 2) - anchor[None, :] + 128
    right, left = (jnp.asarray(t) for t in tables())
    probe = jnp.transpose(probe.reshape(2, 256, 2, 128), (0, 2, 1, 3))
    sides = pltpu.SemaphoreType.DMA((8,))
    ext, arranged = pl.pallas_call(
        halo_kernel,
        out_shape=(EXT, jax.ShapeDtypeStruct((count, 256, 256), BF16)),
        in_specs=[VMEM] * 3,
        out_specs=(VMEM, VMEM),
        scratch_shapes=[sides, sides],
        compiler_params=params(0),
        name="halo",
    )(obj, amps.reshape(count, 256, 256), jnp.asarray(sorting()))
    for step in range(2):
        last = step == 1
        grad, total = pl.pallas_call(
            compute_kernel,
            out_shape=(EXT, jax.ShapeDtypeStruct((3, 2, 256, 128), F32)),
            in_specs=[SMEM] + [VMEM] * 5,
            out_specs=(VMEM, VMEM),
            scratch_shapes=[
                pltpu.VMEM((2, 2, 256, 128), F32),
                pltpu.VMEM((2, 256, 256), BF16),
                pltpu.VMEM((2, 256, 256), BF16),
            ],
            compiler_params=params(),
            name="gradient",
        )(local, ext, probe, arranged, right, left)
        outs = pl.pallas_call(
            functools.partial(step_kernel, last),
            out_shape=(TILE, TILE) if last else (EXT, BLOCKS),
            in_specs=[VMEM] * 4,
            out_specs=(VMEM, VMEM),
            scratch_shapes=[
                pltpu.VMEM(EXT.shape, F32),
                pltpu.VMEM(BLOCKS.shape, F32),
                *[sides] * (2 if last else 4),
                *SUM_SCRATCH,
            ],
            compiler_params=params(1 + step),
            name="update",
        )(ext, grad, total.reshape(6, 256, 128), probe)
        ext, probe = outs
    return (ext, probe)


def solution(mesh):
    in_specs = (
        P(None, "gy", "gx"),
        P(),
        P("gy", "gx", None, None),
        P("gy", "gx", None, None, None),
    )
    out_specs = (P(None, "gy", "gx"), P())
    return jax.shard_map(shards, mesh=mesh, in_specs=in_specs, out_specs=out_specs, check_vma=False)
```

```python
import functools

import jax
import jax.numpy as jnp
import ml_dtypes
import numpy as np
from jax import lax
from jax.experimental import pallas as pl
from jax.experimental.pallas import tpu as pltpu
from jax.sharding import PartitionSpec as P

MESH = pl.DeviceIdType.MESH
F32 = jnp.float32
BF16 = jnp.bfloat16
VMEM = pl.BlockSpec(memory_space=pltpu.VMEM)
SMEM = pl.BlockSpec(memory_space=pltpu.SMEM)
VMEM_LIMIT = 60 * 1024 * 1024

DIRS = [(-1, 0), (1, 0), (0, -1), (0, 1), (-1, -1), (-1, 1), (1, -1), (1, 1)]


def tables():
    n = np.arange(128)[:, None]
    out = []
    for parity in range(2):
        turns = (n * (2 * np.arange(128)[None, :] + parity)) % 256
        angle = -2.0 * np.pi * turns / 256.0
        re, im = np.cos(angle) / 16.0, np.sin(angle) / 16.0
        m = np.block([[re, im], [-im, re]]).astype(np.float32)
        hi = m.astype(ml_dtypes.bfloat16)
        lo = (m - hi.astype(np.float32)).astype(ml_dtypes.bfloat16)
        out.append(np.stack([hi, lo]))
    right = np.stack(out)
    return right, np.ascontiguousarray(np.swapaxes(right, 2, 3))


def sorting():
    m = np.zeros((256, 256), np.float32)
    m[np.arange(256), np.concatenate([np.arange(0, 256, 2), np.arange(1, 256, 2)])] = 1.0
    return np.stack([m, m.T]).astype(ml_dtypes.bfloat16)


def neighbor(dy, dx):
    y = lax.axis_index("gy") + dy
    x = lax.axis_index("gx") + dx
    ny, nx = lax.axis_size("gy"), lax.axis_size("gx")
    ok = (y >= 0) & (y < ny) & (x >= 0) & (x < nx)
    return ok, (jnp.clip(y, 0, ny - 1), jnp.clip(x, 0, nx - 1))


def halo_region(dy, dx):
    rows = {-1: slice(0, 128), 0: slice(128, 384), 1: slice(384, 512)}[dy]
    cols = {-1: slice(0, 1), 0: slice(1, 3), 1: slice(3, 4)}[dx]
    return cols, rows


def edge_region(dy, dx):
    rows = {-1: slice(128, 256), 0: slice(128, 384), 1: slice(256, 384)}[dy]
    cols = {-1: slice(1, 2), 0: slice(1, 3), 1: slice(2, 3)}[dx]
    return cols, rows


def greet_sides():
    barrier = pltpu.get_barrier_semaphore()
    count = jnp.int32(0)
    for d in DIRS:
        ok, device = neighbor(*d)

        @pl.when(ok)
        def _(device=device):
            pl.semaphore_signal(barrier, inc=1, device_id=device, device_id_type=MESH)

        count = count + ok.astype(jnp.int32)
    return barrier, count


def side_copies(source, target, outward, send, recv):
    out = []
    for i, (dy, dx) in enumerate(DIRS):
        ok, device = neighbor(dy, dx)
        cols, rows = edge_region(dy, dx) if outward else halo_region(dy, dx)
        tcols, trows = halo_region(-dy, -dx) if outward else (cols, rows)
        out.append(
            (
                ok,
                neighbor(-dy, -dx)[0],
                pltpu.make_async_remote_copy(
                    source.at[:, cols, rows, :],
                    target.at[:, tcols, trows, :],
                    send.at[i],
                    recv.at[i],
                    device_id=device,
                    device_id_type=MESH,
                ),
            )
        )
    return out


def start_sides(copies):
    for ok, _, copy in copies:
        pl.when(ok)(copy.start)


def wait_sides(copies):
    for ok, arrives, copy in copies:
        pl.when(ok)(copy.wait_send)
        pl.when(arrives)(copy.wait_recv)


def blank_outside(ext):
    for dy, dx in DIRS:
        cols, rows = halo_region(dy, dx)

        @pl.when(jnp.logical_not(neighbor(dy, dx)[0]))
        def _(cols=cols, rows=rows):
            ext[:, cols, rows, :] = jnp.zeros((2, cols.stop - cols.start, rows.stop - rows.start, 128), F32)


def arrange(amps, sort, out):
    def one(k, carry):
        half = jnp.dot(sort[0], amps[0, 0, k], preferred_element_type=F32).astype(BF16)
        out[k] = jnp.dot(half, sort[1], preferred_element_type=F32).astype(BF16)
        return carry

    lax.fori_loop(0, out.shape[0], one, jnp.int32(0))


def split(x):
    hi = x.astype(BF16)
    return hi, (x - hi.astype(F32)).astype(BF16)


def right_dot(hi, lo, m):
    return jnp.dot(
        jnp.concatenate([hi, lo, hi], axis=1),
        jnp.concatenate([m[0], m[0], m[1]], axis=0),
        preferred_element_type=F32,
    )


def left_dot(m, hi, lo):
    return jnp.dot(
        jnp.concatenate([m[0], m[0], m[1]], axis=1),
        jnp.concatenate([hi, lo, hi], axis=0),
        preferred_element_type=F32,
    )


def gradients(positions, ext, probe, amps, right, left, grad, total, cut, lhs_hi, lhs_lo, stage):
    total[...] = jnp.zeros_like(total)
    row0 = lax.axis_index("gy") * 256 - 128
    col0 = lax.axis_index("gx") * 256 - 128

    def corner(k):
        return jnp.clip(positions[0, 0, k, 0] - row0, 0, 255), jnp.clip(positions[0, 0, k, 1] - col0, 0, 255)

    lane = lax.broadcasted_iota(jnp.int32, (1, 128), 1)

    def visit(k, carry):
        r, c = corner(k)
        first = lax.div(c, 128)
        c = lax.rem(c, 128)
        back = lax.rem(128 - c, 128)
        keep = lane < 128 - c
        late = lane >= c
        for i in range(0, 256, 64):
            rows = slice(i, i + 64)
            part = []
            for p in range(2):
                t = [pltpu.roll(ext[p, first + b, pl.ds(r + i, 64), :], back, 1) for b in range(3)]
                h = [jnp.where(keep, t[0], t[1]), jnp.where(keep, t[1], t[2])]
                for b in range(2):
                    cut[p, b, rows, :] = h[b]
                part.append(h)
            wave = []
            for b in range(2):
                ore, oim = part[0][b], part[1][b]
                pre, pim = probe[0, b, rows, :], probe[1, b, rows, :]
                total[4 + b, rows, :] += ore * ore + oim * oim
                wave.append((pre * ore - pim * oim, pre * oim + pim * ore))
            for q in range(2):
                for p in range(2):
                    x = wave[0][p] + wave[1][p] if q == 0 else wave[0][p] - wave[1][p]
                    hi, lo = split(x)
                    lhs_hi[q, rows, 128 * p : 128 * p + 128] = hi
                    lhs_lo[q, rows, 128 * p : 128 * p + 128] = lo
        y = [right_dot(lhs_hi[q], lhs_lo[q], right[q]) for q in range(2)]
        half = []
        for s in range(2):
            pieces = []
            for p in range(2):
                lanes = slice(128 * p, 128 * p + 128)
                top = jnp.concatenate([y[0][:128, lanes], y[1][:128, lanes]], axis=1)
                low = jnp.concatenate([y[0][128:, lanes], y[1][128:, lanes]], axis=1)
                pieces.append(top + low if s == 0 else top - low)
            hi, lo = split(jnp.concatenate(pieces, axis=0))
            far = left_dot(left[s], hi, lo)
            re, im = far[:128], far[128:]
            factor = amps[k, 128 * s : 128 * s + 128, :].astype(F32) * lax.rsqrt(jnp.maximum(re * re + im * im, 0.25)) - 1.0
            hi, lo = split(jnp.concatenate([re * factor, im * factor], axis=0))
            half.append(left_dot(right[s], hi, lo))
        top, low = half[0] + half[1], half[0] - half[1]
        chi = []
        for q in range(2):
            lanes = slice(128 * q, 128 * q + 128)
            x = jnp.concatenate(
                [
                    jnp.concatenate([top[:128, lanes], top[128:, lanes]], axis=1),
                    jnp.concatenate([low[:128, lanes], low[128:, lanes]], axis=1),
                ],
                axis=0,
            )
            hi, lo = split(x)
            chi.append(right_dot(hi, lo, left[q]))
        for i in range(0, 256, 64):
            rows = slice(i, i + 64)
            g = [[], []]
            for b in range(2):
                x = chi[0][rows] + chi[1][rows] if b == 0 else chi[0][rows] - chi[1][rows]
                cre, cim = x[:, :128], x[:, 128:]
                pre, pim = probe[0, b, rows, :], probe[1, b, rows, :]
                ore, oim = cut[0, b, rows, :], cut[1, b, rows, :]
                total[b, rows, :] += ore * cre + oim * cim
                total[2 + b, rows, :] += ore * cim - oim * cre
                g[0].append(pltpu.roll(pre * cre + pim * cim, c, 1))
                g[1].append(pltpu.roll(pre * cim - pim * cre, c, 1))
            for p in range(2):
                place = slice(256 + i, 320 + i)
                stage[k, p, 1, place, :] = jnp.where(late, g[p][0], 0.0)
                stage[k, p, 2, place, :] = jnp.where(late, g[p][1], g[p][0])
                stage[k, p, 3, place, :] = jnp.where(late, 0.0, g[p][1])
        return carry

    lax.fori_loop(0, amps.shape[0], visit, jnp.int32(0))

    def gather(i, carry):
        start = pl.multiple_of(i * 64, 64)
        for p in range(2):
            for b in range(4):
                x = jnp.zeros((64, 128), F32)
                for k in range(amps.shape[0]):
                    r, c = corner(k)
                    first = lax.div(c, 128)
                    x = x + stage[k, p, b + 1 - first, pl.ds(256 + start - r, 64), :]
                grad[p, b, pl.ds(start, 64), :] = x
        return carry

    lax.fori_loop(0, 8, gather, jnp.int32(0))


def group_ids():
    gy, gx = lax.axis_index("gy"), lax.axis_index("gx")
    return lax.rem(gx, 2), lax.rem(gy, 4), lax.div(gy, 4) * 8 + lax.div(gx, 2)


def sibling():
    gy, gx = lax.axis_index("gy"), lax.axis_index("gx")
    return gy, gx + 1 - 2 * lax.rem(gx, 2)


def along_y(d):
    gy, gx = lax.axis_index("gy"), lax.axis_index("gx")
    y = lax.rem(gy, 4)
    return gy - y + lax.rem(y + d, 4), gx


def member(j):
    gy, gx = lax.axis_index("gy"), lax.axis_index("gx")
    return lax.div(j, 8) * 4 + lax.rem(gy, 4), lax.rem(j, 8) * 2 + lax.rem(gx, 2)


class Sum:
    def __init__(self, total, full, acc0, acc1, acc2, rb0, rb1, rb2, sems):
        self.total, self.full, self.acc0, self.acc1, self.acc2 = total, full, acc0, acc1, acc2
        self.rb0, self.rb1, self.rb2 = rb0, rb1, rb2
        self.sems = sems
        self.core, self.y, self.me = group_ids()
        self.mine = lax.rem(self.me, 8)

    def greet(self, barrier):
        devices = [sibling()] + [along_y(d) for d in (1, 2, 3)] + [member(lax.rem(self.me + d, 16)) for d in range(1, 16)]
        for device in devices:
            pl.semaphore_signal(barrier, inc=1, device_id=device, device_id_type=MESH)
        return len(devices)

    def copy(self, source, target, i, j, device):
        send, recv = self.sems
        return pltpu.make_async_remote_copy(
            source, target, send.at[i], recv.at[j], device_id=device, device_id_type=MESH
        )

    def step0(self):
        theirs = pl.ds(pl.multiple_of((1 - self.core) * 128, 128), 128)
        self.c0 = self.copy(self.total.at[:, theirs, :], self.rb0, 0, 0, sibling())
        self.c0.start()

    def step1(self):
        self.c0.wait_recv()
        own = pl.ds(pl.multiple_of(self.core * 128, 128), 128)
        self.acc0[...] = self.total[:, own, :] + self.rb0[...]
        self.c1 = []
        for d in (1, 2, 3):
            part = pl.ds(pl.multiple_of(lax.rem(self.y + d, 4) * 32, 32), 32)
            c = self.copy(self.acc0.at[:, part, :], self.rb1.at[d - 1], d, d, along_y(d))
            c.start()
            self.c1.append(c)

    def step2(self):
        for c in self.c1:
            c.wait_recv()
        own = pl.ds(pl.multiple_of(self.y * 32, 32), 32)
        x = self.acc0[:, own, :] + self.rb1[0] + self.rb1[1] + self.rb1[2]
        self.acc1[...] = x.reshape(24, 8, 128)
        self.rb2[pl.ds(self.me, 1)] = self.acc1[pl.ds(self.mine * 3, 3)][None]
        self.c2 = []
        for d in range(1, 16):
            to = lax.rem(self.me + d, 16)
            c = self.copy(
                self.acc1.at[pl.ds(lax.rem(to, 8) * 3, 3)], self.rb2.at[self.me], 3 + d, 3 + d, member(to)
            )
            c.start()
            self.c2.append(c)

    def step3(self):
        for c in self.c2:
            c.wait_recv()
        x = self.rb2[0]
        for j in range(1, 16):
            x = x + self.rb2[j]
        self.acc2[...] = x
        place = self.full.at[self.core, self.y, pl.ds(self.mine * 3, 3)]
        self.full[pl.ds(self.core, 1), pl.ds(self.y, 1), pl.ds(self.mine * 3, 3)] = x[None, None]
        self.c3 = []
        for d in range(1, 8):
            to = lax.rem(self.mine + d, 8) + lax.div(self.me, 8) * 8
            c = self.copy(self.acc2, place, 18 + d, 18 + d, member(to))
            c.start()
            self.c3.append(c)

    def step4(self):
        for c in self.c3:
            c.wait_recv()
        self.c4 = []
        for d in (1, 2, 3):
            place = self.full.at[self.core, self.y]
            c = self.copy(place, place, 25 + d, 25 + d, along_y(d))
            c.start()
            self.c4.append(c)

    def step5(self):
        for c in self.c4:
            c.wait_recv()
        place = self.full.at[self.core]
        self.c5 = self.copy(place, place, 29, 29, sibling())
        self.c5.start()

    def finish(self):
        self.c5.wait_recv()
        for c in [self.c0, *self.c1, *self.c2, *self.c3, *self.c4, self.c5]:
            c.wait_send()


SUM_SCRATCH = [
    pltpu.VMEM((2, 4, 24, 8, 128), F32),
    pltpu.VMEM((6, 128, 128), F32),
    pltpu.VMEM((24, 8, 128), F32),
    pltpu.VMEM((3, 8, 128), F32),
    pltpu.VMEM((6, 128, 128), F32),
    pltpu.VMEM((3, 6, 32, 128), F32),
    pltpu.VMEM((16, 3, 8, 128), F32),
    pltpu.SemaphoreType.DMA((30,)),
    pltpu.SemaphoreType.DMA((30,)),
]


def new_probe(probe, full, write):
    weights = [full[h, y, 16:24] for h in range(2) for y in range(4)]
    top = weights[0]
    for w in weights[1:]:
        top = jnp.maximum(top, w)
    floor = 0.1 * jnp.max(top)
    for h in range(2):
        for y in range(4):
            rows = slice(128 * h + 32 * y, 128 * h + 32 * y + 32)
            for b in range(2):
                w = 0.9 * full[h, y, 16 + 4 * b : 20 + 4 * b].reshape(32, 128) + floor
                for p in range(2):
                    g = full[h, y, 8 * p + 4 * b : 8 * p + 4 * b + 4].reshape(32, 128)
                    write(p, b, rows, probe[p, b, rows, :] + g / w)


def kernel(positions, obj, probe, amps, right, left, sort, obj_out, probe_out, *refs):
    ext, grad, total, acc, probes, arranged, cut, lhs_hi, lhs_lo, stage, inbox, send, recv, *rest = refs
    sums = []
    for step in range(2):
        parts = rest[len(SUM_SCRATCH) * step : len(SUM_SCRATCH) * (step + 1)]
        sums.append(Sum(total, *parts[:-2], parts[-2:]))
    for step in range(2):
        blank_outside(ext.at[step])
    barrier, count = greet_sides()
    count = count + sums[0].greet(barrier)
    for b in range(2):
        lanes = slice(128 * b, 128 * b + 128)
        ext[0, :, 1 + b, 128:384, :] = obj[:, :, lanes]
        probes[0, :, b] = probe[:, :, lanes]
    pl.semaphore_wait(barrier, count)
    copies = side_copies(ext.at[0], ext.at[0], True, send.at[0], recv.at[0])
    start_sides(copies)
    arrange(amps, sort, arranged)

    def clear(k, carry):
        for p in range(2):
            for b in range(5):
                for rows in (slice(0, 256), slice(256, 512), slice(512, 768)):
                    if b in (0, 4) or rows.start != 256:
                        stage[k, p, b, rows, :] = jnp.zeros((256, 128), F32)
        return carry

    lax.fori_loop(0, stage.shape[0], clear, jnp.int32(0))
    wait_sides(copies)
    for step in range(2):
        adder = sums[step]
        old, now = ext.at[step], probes.at[step]
        gradients(positions, old, now, arranged, right, left, grad, total, cut, lhs_hi, lhs_lo, stage)
        adder.step0()
        copies = side_copies(grad, inbox.at[step], False, send.at[1 + 2 * step], recv.at[1 + 2 * step])
        start_sides(copies)
        peak = jnp.max(now[0] * now[0] + now[1] * now[1])
        adder.step1()
        acc[...] = grad[:, 1:3, 128:384, :]
        adder.step2()
        wait_sides(copies)
        for dy, dx in DIRS:
            cols, rows = halo_region(dy, dx)
            tcols, trows = edge_region(-dy, -dx)

            @pl.when(neighbor(-dy, -dx)[0])
            def _(cols=cols, rows=rows, tcols=tcols, trows=trows):
                place = (slice(None), slice(tcols.start - 1, tcols.stop - 1), slice(trows.start - 128, trows.stop - 128))
                acc[place] += inbox[step, :, cols, rows, :]

        if step == 1:
            for b in range(2):
                obj_out[:, :, 128 * b : 128 * b + 128] = old[:, 1 + b, 128:384, :] + acc[:, b] / peak
        else:
            ext[1, :, 1:3, 128:384, :] = old[:, 1:3, 128:384, :] + acc[...] / peak
            copies = side_copies(ext.at[1], ext.at[1], True, send.at[2], recv.at[2])
            start_sides(copies)
        adder.step3()
        adder.step4()
        adder.step5()
        adder.finish()

        def write(p, b, rows, x):
            if step == 1:
                probe_out[p, rows, 128 * b : 128 * b + 128] = x
            else:
                probes[1, p, b, rows, :] = x

        new_probe(now, adder.full, write)
        if step == 0:
            wait_sides(copies)


def shards(obj, probe, positions, amps):
    count = positions.shape[2]
    right, left = (jnp.asarray(t) for t in tables())
    tile = jax.ShapeDtypeStruct((2, 256, 256), F32)
    ext = (2, 4, 512, 128)
    return pl.pallas_call(
        kernel,
        out_shape=(tile, tile),
        in_specs=[SMEM] + [VMEM] * 6,
        out_specs=(VMEM, VMEM),
        scratch_shapes=[
            pltpu.VMEM((2, *ext), F32),
            pltpu.VMEM(ext, F32),
            pltpu.VMEM((6, 256, 128), F32),
            pltpu.VMEM((2, 2, 256, 128), F32),
            pltpu.VMEM((2, 2, 2, 256, 128), F32),
            pltpu.VMEM((count, 256, 256), BF16),
            pltpu.VMEM((2, 2, 256, 128), F32),
            pltpu.VMEM((2, 256, 256), BF16),
            pltpu.VMEM((2, 256, 256), BF16),
            pltpu.VMEM((count, 2, 5, 768, 128), F32),
            pltpu.VMEM((2, *ext), F32),
            pltpu.SemaphoreType.DMA((4, 8)),
            pltpu.SemaphoreType.DMA((4, 8)),
            *SUM_SCRATCH,
            *SUM_SCRATCH,
        ],
        compiler_params=pltpu.CompilerParams(collective_id=0, has_side_effects=True, vmem_limit_bytes=VMEM_LIMIT),
        name="iterations",
    )(positions, obj, probe, amps, right, left, jnp.asarray(sorting()))


def solution(mesh):
    in_specs = (
        P(None, "gy", "gx"),
        P(),
        P("gy", "gx", None, None),
        P("gy", "gx", None, None, None),
    )
    out_specs = (P(None, "gy", "gx"), P())
    return jax.shard_map(shards, mesh=mesh, in_specs=in_specs, out_specs=out_specs, check_vma=False)
```

```python
import functools

import jax
import jax.numpy as jnp
import ml_dtypes
import numpy as np
from jax import lax
from jax.experimental import pallas as pl
from jax.experimental.pallas import tpu as pltpu
from jax.sharding import PartitionSpec as P

MESH = pl.DeviceIdType.MESH
F32 = jnp.float32
BF16 = jnp.bfloat16
VMEM = pl.BlockSpec(memory_space=pltpu.VMEM)
SMEM = pl.BlockSpec(memory_space=pltpu.SMEM)
VMEM_LIMIT = 60 * 1024 * 1024

DIRS = [(-1, 0), (1, 0), (0, -1), (0, 1), (-1, -1), (-1, 1), (1, -1), (1, 1)]


def tables():
    n = np.arange(128)[:, None]
    out = []
    for parity in range(2):
        turns = (n * (2 * np.arange(128)[None, :] + parity)) % 256
        angle = -2.0 * np.pi * turns / 256.0
        re, im = np.cos(angle) / 16.0, np.sin(angle) / 16.0
        m = np.block([[re, im], [-im, re]]).astype(np.float32)
        hi = m.astype(ml_dtypes.bfloat16)
        lo = (m - hi.astype(np.float32)).astype(ml_dtypes.bfloat16)
        out.append(np.stack([hi, lo]))
    right = np.stack(out)
    return right, np.ascontiguousarray(np.swapaxes(right, 2, 3))


def sorting():
    m = np.zeros((256, 256), np.float32)
    m[np.arange(256), np.concatenate([np.arange(0, 256, 2), np.arange(1, 256, 2)])] = 1.0
    return np.stack([m, m.T]).astype(ml_dtypes.bfloat16)


def neighbor(dy, dx):
    y = lax.axis_index("gy") + dy
    x = lax.axis_index("gx") + dx
    ny, nx = lax.axis_size("gy"), lax.axis_size("gx")
    ok = (y >= 0) & (y < ny) & (x >= 0) & (x < nx)
    return ok, (jnp.clip(y, 0, ny - 1), jnp.clip(x, 0, nx - 1))


def halo_region(dy, dx):
    rows = {-1: slice(0, 128), 0: slice(128, 384), 1: slice(384, 512)}[dy]
    cols = {-1: slice(0, 1), 0: slice(1, 3), 1: slice(3, 4)}[dx]
    return cols, rows


def edge_region(dy, dx):
    rows = {-1: slice(128, 256), 0: slice(128, 384), 1: slice(256, 384)}[dy]
    cols = {-1: slice(1, 2), 0: slice(1, 3), 1: slice(2, 3)}[dx]
    return cols, rows


def greet_sides():
    barrier = pltpu.get_barrier_semaphore()
    count = jnp.int32(0)
    for d in DIRS:
        ok, device = neighbor(*d)

        @pl.when(ok)
        def _(device=device):
            pl.semaphore_signal(barrier, inc=1, device_id=device, device_id_type=MESH)

        count = count + ok.astype(jnp.int32)
    return barrier, count


def side_copies(source, target, outward, send, recv):
    out = []
    for i, (dy, dx) in enumerate(DIRS):
        ok, device = neighbor(dy, dx)
        cols, rows = edge_region(dy, dx) if outward else halo_region(dy, dx)
        tcols, trows = halo_region(-dy, -dx) if outward else (cols, rows)
        out.append(
            (
                ok,
                neighbor(-dy, -dx)[0],
                pltpu.make_async_remote_copy(
                    source.at[:, cols, rows, :],
                    target.at[:, tcols, trows, :],
                    send.at[i],
                    recv.at[i],
                    device_id=device,
                    device_id_type=MESH,
                ),
            )
        )
    return out


def start_sides(copies):
    for ok, _, copy in copies:
        pl.when(ok)(copy.start)


def wait_sides(copies):
    for ok, arrives, copy in copies:
        pl.when(ok)(copy.wait_send)
        pl.when(arrives)(copy.wait_recv)


def blank_outside(ext):
    for dy, dx in DIRS:
        cols, rows = halo_region(dy, dx)

        @pl.when(jnp.logical_not(neighbor(dy, dx)[0]))
        def _(cols=cols, rows=rows):
            ext[:, cols, rows, :] = jnp.zeros((2, cols.stop - cols.start, rows.stop - rows.start, 128), F32)


def arrange(amps, sort, out):
    def one(k, carry):
        half = jnp.dot(sort[0], amps[0, 0, k], preferred_element_type=F32).astype(BF16)
        out[k] = jnp.dot(half, sort[1], preferred_element_type=F32).astype(BF16)
        return carry

    lax.fori_loop(0, out.shape[0], one, jnp.int32(0))


def split(x):
    hi = x.astype(BF16)
    return hi, (x - hi.astype(F32)).astype(BF16)


def right_dot(hi, lo, m):
    return jnp.dot(
        jnp.concatenate([hi, lo, hi], axis=1),
        jnp.concatenate([m[0], m[0], m[1]], axis=0),
        preferred_element_type=F32,
    )


def left_dot(m, hi, lo):
    return jnp.dot(
        jnp.concatenate([m[0], m[0], m[1]], axis=1),
        jnp.concatenate([hi, lo, hi], axis=0),
        preferred_element_type=F32,
    )


def corner(positions, k):
    row = positions[0, 0, k, 0] - lax.axis_index("gy") * 256 + 128
    col = positions[0, 0, k, 1] - lax.axis_index("gx") * 256 + 128
    return jnp.clip(row, 0, 255), jnp.clip(col, 0, 255)


def cut_patches(positions, ext, cut, total):
    total[4:6] = jnp.zeros((2, 256, 128), F32)
    lane = lax.broadcasted_iota(jnp.int32, (1, 128), 1)

    def visit(k, carry):
        r, c = corner(positions, k)
        first = lax.div(c, 128)
        c = lax.rem(c, 128)
        back = lax.rem(128 - c, 128)
        keep = lane < 128 - c
        for i in range(0, 256, 64):
            rows = slice(i, i + 64)
            part = []
            for p in range(2):
                t = [pltpu.roll(ext[p, first + b, pl.ds(r + i, 64), :], back, 1) for b in range(3)]
                h = [jnp.where(keep, t[0], t[1]), jnp.where(keep, t[1], t[2])]
                for b in range(2):
                    cut[k, p, b, rows, :] = h[b]
                part.append(h)
            for b in range(2):
                total[4 + b, rows, :] += part[0][b] * part[0][b] + part[1][b] * part[1][b]
        return carry

    lax.fori_loop(0, cut.shape[0], visit, jnp.int32(0))


def gradients(positions, cut, probe, amps, right, left, total, lhs_hi, lhs_lo, chi, stage):
    total[0:4] = jnp.zeros((4, 256, 128), F32)
    chi[...] = jnp.zeros_like(chi)
    lane = lax.broadcasted_iota(jnp.int32, (1, 128), 1)
    pairs = cut.shape[0] // 2

    def waves(k, u):
        for i in range(0, 256, 64):
            rows = slice(i, i + 64)
            place = slice(256 * u + i, 256 * u + i + 64)
            wave = []
            for b in range(2):
                ore, oim = cut[k, 0, b, rows, :], cut[k, 1, b, rows, :]
                pre, pim = probe[0, b, rows, :], probe[1, b, rows, :]
                wave.append((pre * ore - pim * oim, pre * oim + pim * ore))
            for q in range(2):
                for p in range(2):
                    x = wave[0][p] + wave[1][p] if q == 0 else wave[0][p] - wave[1][p]
                    hi, lo = split(x)
                    lhs_hi[q, place, 128 * p : 128 * p + 128] = hi
                    lhs_lo[q, place, 128 * p : 128 * p + 128] = lo

    def correct(k, s, top, low):
        hi, lo = split(top + low if s == 0 else top - low)
        far = left_dot(left[s], hi, lo)
        re, im = far[:128], far[128:]
        factor = amps[k, 128 * s : 128 * s + 128, :].astype(F32) * lax.rsqrt(jnp.maximum(re * re + im * im, 0.25)) - 1.0
        hi, lo = split(jnp.concatenate([re * factor, im * factor], axis=0))
        return left_dot(right[s], hi, lo)

    def deposit(k, u):
        c = lax.rem(corner(positions, k)[1], 128)
        late = lane >= c
        for i in range(0, 256, 64):
            rows = slice(i, i + 64)
            place = slice(256 * u + i, 256 * u + i + 64)
            even, odd = chi[0, place, :], chi[1, place, :]
            g = [[], []]
            for b in range(2):
                x = even + odd if b == 0 else even - odd
                cre, cim = x[:, :128], x[:, 128:]
                pre, pim = probe[0, b, rows, :], probe[1, b, rows, :]
                ore, oim = cut[k, 0, b, rows, :], cut[k, 1, b, rows, :]
                total[b, rows, :] += ore * cre + oim * cim
                total[2 + b, rows, :] += ore * cim - oim * cre
                g[0].append(pltpu.roll(pre * cre + pim * cim, c, 1))
                g[1].append(pltpu.roll(pre * cim - pim * cre, c, 1))
            for p in range(2):
                to = pl.ds(pl.multiple_of(512 * k + 256 + i, 64), 64)
                stage[p, 1, to, :] = jnp.where(late, g[p][0], 0.0)
                stage[p, 2, to, :] = jnp.where(late, g[p][1], g[p][0])
                stage[p, 3, to, :] = jnp.where(late, 0.0, g[p][1])

    def stack(y, u):
        out = []
        for h in range(2):
            rows = slice(256 * u + 128 * h, 256 * u + 128 * h + 128)
            parts = [
                jnp.concatenate([y[0][rows, lanes], y[1][rows, lanes]], axis=1)
                for lanes in (slice(0, 128), slice(128, 256))
            ]
            out.append(jnp.concatenate(parts, axis=0))
        return out

    def visit(j, carry):
        y = [right_dot(lhs_hi[q], lhs_lo[q], right[q]) for q in range(2)]
        for u in range(2):
            deposit(2 * jnp.maximum(j - 1, 0) + u, u)
        half = [[], []]
        for s in range(2):
            for u in range(2):
                top, low = stack(y, u)
                half[u].append(correct(2 * j + u, s, top, low))
        for q in range(2):
            lanes = slice(128 * q, 128 * q + 128)
            parts = []
            for u in range(2):
                for x in (half[u][0] + half[u][1], half[u][0] - half[u][1]):
                    parts.append(jnp.concatenate([x[:128, lanes], x[128:, lanes]], axis=1))
            hi, lo = split(jnp.concatenate(parts, axis=0))
            chi[q] = right_dot(hi, lo, left[q])
        for u in range(2):
            waves(2 * jnp.minimum(j + 1, pairs - 1) + u, u)
        return carry

    for u in range(2):
        waves(u, u)
    lax.fori_loop(0, pairs, visit, jnp.int32(0))
    for u in range(2):
        deposit(2 * pairs - 2 + u, u)


def gather(positions, stage, grad, cols, rows):
    def part(i, carry):
        start = pl.multiple_of(i * 64, 64)
        for p in range(2):
            for b in cols:
                x = jnp.zeros((64, 128), F32)
                for k in range(stage.shape[2] // 512):
                    r, c = corner(positions, k)
                    x = x + stage[p, lax.rem(b + 1 - lax.div(c, 128), 4), pl.ds(512 * k + 256 + start - r, 64), :]
                grad[p, b, pl.ds(start, 64), :] = x
        return carry

    lax.fori_loop(rows.start // 64, rows.stop // 64, part, jnp.int32(0))


def sibling():
    gy, gx = lax.axis_index("gy"), lax.axis_index("gx")
    return gy, gx + 1 - 2 * lax.rem(gx, 2)


def along_x(d):
    gy, gx = lax.axis_index("gy"), lax.axis_index("gx")
    x = lax.div(gx, 4)
    return gy, lax.rem(x + d, 4) * 4 + lax.rem(gx, 4)


def member(j):
    gx = lax.axis_index("gx")
    place = lax.rem(j, 8)
    return lax.div(j, 8) * 4 + lax.div(place, 2), lax.div(gx, 4) * 4 + lax.rem(place, 2) * 2 + lax.rem(gx, 2)


class Sum:
    def __init__(self, total, full, acc0, acc1, acc2, rb0, rb1, rb2, send, recv):
        self.total, self.full, self.acc0, self.acc1, self.acc2 = total, full, acc0, acc1, acc2
        self.rb0, self.rb1, self.rb2 = rb0, rb1, rb2
        self.send, self.recv = send, recv
        gy, gx = lax.axis_index("gy"), lax.axis_index("gx")
        self.core, self.x = lax.rem(gx, 2), lax.div(gx, 4)
        self.mine = lax.rem(gy, 4) * 2 + lax.div(lax.rem(gx, 4), 2)
        self.me = lax.div(gy, 4) * 8 + self.mine
        self.tiles = total.shape[0] // 2

    def greet(self, barrier):
        devices = [sibling()] + [along_x(d) for d in (1, 2, 3)] + [member(lax.rem(self.me + d, 16)) for d in range(1, 16)]
        for device in devices:
            pl.semaphore_signal(barrier, inc=1, device_id=device, device_id_type=MESH)
        return len(devices)

    def copy(self, source, target, i, device):
        return pltpu.make_async_remote_copy(
            source, target, self.send.at[i], self.recv.at[i], device_id=device, device_id_type=MESH
        )

    def copies0(self):
        theirs = pl.ds(pl.multiple_of((1 - self.core) * 128, 128), 128)
        return [self.copy(self.total.at[:, theirs, :], self.rb0, 0, sibling())]

    def copies1(self):
        out = []
        for d in (1, 2, 3):
            part = pl.ds(pl.multiple_of(lax.rem(self.x + d, 4) * 32, 32), 32)
            out.append(self.copy(self.acc0.at[:, part, :], self.rb1.at[d - 1], d, along_x(d)))
        return out

    def copies2(self):
        out = []
        for d in range(1, 16):
            to = lax.rem(self.me + d, 16)
            part = pl.ds(lax.rem(to, 8) * self.tiles, self.tiles)
            out.append(self.copy(self.acc1.at[part], self.rb2.at[self.me], 3 + d, member(to)))
        return out

    def copies3(self):
        place = self.full.at[self.core, self.x, pl.ds(self.mine * self.tiles, self.tiles)]
        out = []
        for d in range(1, 8):
            to = lax.rem(self.mine + d, 8) + lax.div(self.me, 8) * 8
            out.append(self.copy(self.acc2, place, 18 + d, member(to)))
        return out

    def copies4(self):
        place = self.full.at[self.core, self.x]
        return [self.copy(place, place, 25 + d, along_x(d)) for d in (1, 2, 3)]

    def copies5(self):
        place = self.full.at[self.core]
        return [self.copy(place, place, 29, sibling())]

    def step(self, number):
        if number > 0:
            for c in getattr(self, f"copies{number - 1}")():
                c.wait_recv()
        if number == 1:
            own = pl.ds(pl.multiple_of(self.core * 128, 128), 128)
            self.acc0[...] = self.total[:, own, :] + self.rb0[...]
        if number == 2:
            own = pl.ds(pl.multiple_of(self.x * 32, 32), 32)
            x = self.acc0[:, own, :] + self.rb1[0] + self.rb1[1] + self.rb1[2]
            self.acc1[...] = x.reshape(self.acc1.shape)
            self.rb2[pl.ds(self.me, 1)] = self.acc1[pl.ds(self.mine * self.tiles, self.tiles)][None]
        if number == 3:
            x = self.rb2[0]
            for j in range(1, 16):
                x = x + self.rb2[j]
            self.acc2[...] = x
            self.full[pl.ds(self.core, 1), pl.ds(self.x, 1), pl.ds(self.mine * self.tiles, self.tiles)] = x[None, None]
        if number < 6:
            for c in getattr(self, f"copies{number}")():
                c.start()
        else:
            for stage in range(6):
                for c in getattr(self, f"copies{stage}")():
                    c.wait_send()


def sum_scratch(n):
    return [
        pltpu.VMEM((2, 4, 4 * n, 8, 128), F32),
        pltpu.VMEM((n, 128, 128), F32),
        pltpu.VMEM((4 * n, 8, 128), F32),
        pltpu.VMEM((n // 2, 8, 128), F32),
        pltpu.VMEM((n, 128, 128), F32),
        pltpu.VMEM((3, n, 32, 128), F32),
        pltpu.VMEM((16, n // 2, 8, 128), F32),
        pltpu.SemaphoreType.DMA((30,)),
        pltpu.SemaphoreType.DMA((30,)),
    ]


def new_probe(probe, full, write):
    parts = [full[h, x, 16:24] for h in range(2) for x in range(4)]
    top = parts[0]
    for w in parts[1:]:
        top = jnp.maximum(top, w)
    floor = 0.1 * jnp.max(top)
    for h in range(2):
        for x in range(4):
            rows = slice(128 * h + 32 * x, 128 * h + 32 * x + 32)
            for b in range(2):
                w = 0.9 * full[h, x, 16 + 4 * b : 20 + 4 * b].reshape(32, 128) + floor
                for p in range(2):
                    g = full[h, x, 8 * p + 4 * b : 8 * p + 4 * b + 4].reshape(32, 128)
                    write(p, b, rows, probe[p, b, rows, :] + g / w)


ORDERS = (
    ("s0", "gy", "s1", "y", "gx", "go", "s2", "x", "s3", "d", "s4", "w", "u", "cy", "s5", "cx", "cd", "s6", "p", "cw"),
    ("s0", "gy", "s1", "y", "gx", "go", "s2", "x", "s3", "d", "s4", "w", "u", "s5", "s6", "p"),
)


def kernel(positions, obj, probe, amps, right, left, sort, obj_out, probe_out, *refs):
    ext, grad, total, acc, probes, arranged, cut, lhs_hi, lhs_lo, chi, stage, inbox, send, recv, *rest = refs
    size = len(rest) // 2
    sums = [Sum(total, *rest[size * step : size * (step + 1)]) for step in range(2)]
    for step in range(2):
        blank_outside(ext.at[step])
    barrier, count = greet_sides()
    count = count + sums[0].greet(barrier)
    for b in range(2):
        lanes = slice(128 * b, 128 * b + 128)
        ext[0, :, 1 + b, 128:384, :] = obj[:, :, lanes]
        probes[0, :, b] = probe[:, :, lanes]

    def clear(k, carry):
        for p in range(2):
            for b in range(4):
                stage[p, b, pl.ds(pl.multiple_of(512 * k, 512), 256), :] = jnp.zeros((256, 128), F32)
            stage[p, 0, pl.ds(pl.multiple_of(512 * k + 256, 256), 256), :] = jnp.zeros((256, 128), F32)
        return carry

    lax.fori_loop(0, cut.shape[0], clear, jnp.int32(0))
    stage[:, :, 512 * cut.shape[0] :, :] = jnp.zeros((2, 4, 256, 128), F32)
    pl.semaphore_wait(barrier, count)
    copies = side_copies(ext.at[0], ext.at[0], True, send.at[0], recv.at[0])
    start_sides(copies)
    arrange(amps, sort, arranged)
    wait_sides(copies)
    for step in range(2):
        old, now = ext.at[step], probes.at[step]
        cut_patches(positions, old, cut, total)
        gradients(positions, cut, now, arranged, right, left, total, lhs_hi, lhs_lo, chi, stage)
        update(step, positions, stage, grad, inbox.at[step], acc, old, ext.at[1], now, probes.at[1], sums[step], send, recv, obj_out, probe_out)


def update(step, positions, stage, grad, inbox, acc, old, new, now, later, adder, send, recv, obj_out, probe_out):
    peak = jnp.max(now[0] * now[0] + now[1] * now[1])
    inward = side_copies(grad, inbox, False, send.at[1 + 2 * step], recv.at[1 + 2 * step])
    outward = side_copies(new, new, True, send.at[2], recv.at[2])

    def some(copies, kind):
        return [c for c, (dy, dx) in zip(copies, DIRS) if kind == ("d" if dy and dx else "y" if dy else "x")]

    def write(p, b, rows, x):
        if step == 1:
            probe_out[p, rows, 128 * b : 128 * b + 128] = x
        else:
            later[p, b, rows, :] = x

    for event in ORDERS[step]:
        if event == "gy":
            gather(positions, stage, grad, range(4), slice(0, 128))
            gather(positions, stage, grad, range(4), slice(384, 512))
        elif event == "gx":
            gather(positions, stage, grad, (0, 3), slice(128, 384))
        elif event == "go":
            gather(positions, stage, grad, (1, 2), slice(128, 384))
            acc[...] = grad[:, 1:3, 128:384, :]
        elif event in ("y", "x", "d"):
            start_sides(some(inward, event))
        elif event in ("cy", "cx", "cd"):
            start_sides(some(outward, event[1]))
        elif event == "cw":
            wait_sides(outward)
        elif event[0] == "s":
            adder.step(int(event[1]))
        elif event == "w":
            wait_sides(inward)
            for dy, dx in DIRS:
                cols, rows = halo_region(dy, dx)
                tcols, trows = edge_region(-dy, -dx)

                @pl.when(neighbor(-dy, -dx)[0])
                def _(cols=cols, rows=rows, tcols=tcols, trows=trows):
                    place = (slice(None), slice(tcols.start - 1, tcols.stop - 1), slice(trows.start - 128, trows.stop - 128))
                    acc[place] += inbox[:, cols, rows, :]

        elif event == "u" and step == 1:
            for b in range(2):
                obj_out[:, :, 128 * b : 128 * b + 128] = old[:, 1 + b, 128:384, :] + acc[:, b] / peak
        elif event == "u":
            new[:, 1:3, 128:384, :] = old[:, 1:3, 128:384, :] + acc[...] / peak
        else:
            new_probe(now, adder.full, write)


def shards(obj, probe, positions, amps):
    count = positions.shape[2]
    right, left = (jnp.asarray(t) for t in tables())
    tile = jax.ShapeDtypeStruct((2, 256, 256), F32)
    ext = (2, 4, 512, 128)
    return pl.pallas_call(
        kernel,
        out_shape=(tile, tile),
        in_specs=[SMEM] + [VMEM] * 6,
        out_specs=(VMEM, VMEM),
        scratch_shapes=[
            pltpu.VMEM((2, *ext), F32),
            pltpu.VMEM(ext, F32),
            pltpu.VMEM((6, 256, 128), F32),
            pltpu.VMEM((2, 2, 256, 128), F32),
            pltpu.VMEM((2, 2, 2, 256, 128), F32),
            pltpu.VMEM((count, 256, 256), BF16),
            pltpu.VMEM((count, 2, 2, 256, 128), F32),
            pltpu.VMEM((2, 512, 256), BF16),
            pltpu.VMEM((2, 512, 256), BF16),
            pltpu.VMEM((2, 512, 256), F32),
            pltpu.VMEM((2, 4, 512 * count + 256, 128), F32),
            pltpu.VMEM((2, *ext), F32),
            pltpu.SemaphoreType.DMA((4, 8)),
            pltpu.SemaphoreType.DMA((4, 8)),
            *sum_scratch(6) * 2,
        ],
        compiler_params=pltpu.CompilerParams(collective_id=0, has_side_effects=True, vmem_limit_bytes=VMEM_LIMIT),
        name="iterations",
    )(positions, obj, probe, amps, right, left, jnp.asarray(sorting()))


def solution(mesh):
    in_specs = (
        P(None, "gy", "gx"),
        P(),
        P("gy", "gx", None, None),
        P("gy", "gx", None, None, None),
    )
    out_specs = (P(None, "gy", "gx"), P())
    return jax.shard_map(shards, mesh=mesh, in_specs=in_specs, out_specs=out_specs, check_vma=False)
```

```python
import functools

import jax
import jax.numpy as jnp
import ml_dtypes
import numpy as np
from jax import lax
from jax.experimental import pallas as pl
from jax.experimental.pallas import tpu as pltpu
from jax.sharding import PartitionSpec as P

MESH = pl.DeviceIdType.MESH
F32 = jnp.float32
BF16 = jnp.bfloat16
VMEM = pl.BlockSpec(memory_space=pltpu.VMEM)
SMEM = pl.BlockSpec(memory_space=pltpu.SMEM)
VMEM_LIMIT = 60 * 1024 * 1024

TOP, UPPER, LOWER, BOTTOM = (slice(128 * i, 128 * i + 128) for i in range(4))
MIDDLE = slice(128, 384)


def tables():
    n = np.arange(128)[:, None]
    out = []
    for parity in range(2):
        turns = (n * (2 * np.arange(128)[None, :] + parity)) % 256
        angle = -2.0 * np.pi * turns / 256.0
        re, im = np.cos(angle) / 16.0, np.sin(angle) / 16.0
        m = np.block([[re, im], [-im, re]]).astype(np.float32)
        hi = m.astype(ml_dtypes.bfloat16)
        lo = (m - hi.astype(np.float32)).astype(ml_dtypes.bfloat16)
        out.append(np.stack([hi, lo]))
    right = np.stack(out)
    return right, np.ascontiguousarray(np.swapaxes(right, 2, 3))


def sorting():
    m = np.zeros((256, 256), np.float32)
    m[np.arange(256), np.concatenate([np.arange(0, 256, 2), np.arange(1, 256, 2)])] = 1.0
    return np.stack([m, m.T]).astype(ml_dtypes.bfloat16)


def around():
    gy, gx = lax.axis_index("gy"), lax.axis_index("gx")
    core = lax.rem(gx, 2)
    outer = jnp.where(core == 0, gx > 0, gx < lax.axis_size("gx") - 1)
    return core, gy > 0, gy < lax.axis_size("gy") - 1, outer


def devices_around():
    gy, gx = lax.axis_index("gy"), lax.axis_index("gx")
    core = lax.rem(gx, 2)
    ny, nx = lax.axis_size("gy"), lax.axis_size("gx")
    return (
        (jnp.maximum(gy - 1, 0), gx),
        (jnp.minimum(gy + 1, ny - 1), gx),
        (gy, jnp.clip(gx + 2 * core - 1, 0, nx - 1)),
        (gy, gx + 1 - 2 * core),
    )


def greet_sides():
    barrier = pltpu.get_barrier_semaphore()
    count = jnp.int32(0)
    for ok, device in zip(around()[1:], devices_around()):

        @pl.when(ok)
        def _(device=device):
            pl.semaphore_signal(barrier, inc=1, device_id=device, device_id_type=MESH)

        count = count + ok.astype(jnp.int32)
    return barrier, count


def sides(send, recv):
    slots = iter(range(16))

    def link(goes, comes, source, target, device):
        i = next(slots)
        return (
            goes,
            comes,
            pltpu.make_async_remote_copy(
                source, target, send.at[i], recv.at[i], device_id=device, device_id_type=MESH
            ),
        )

    return link


def outward(ext, send, recv):
    core, up, down, outer = around()
    above, below, beside, other = devices_around()
    link = sides(send, recv)
    edge, inner = pl.ds(1 + core, 1), pl.ds(2 - core, 1)
    halo, far = pl.ds(3 * core, 1), pl.ds(3 - 3 * core, 1)
    always = up | jnp.logical_not(up)
    return {
        "y": [
            link(up, down, ext.at[:, 1:3, UPPER], ext.at[:, 1:3, BOTTOM], above),
            link(down, up, ext.at[:, 1:3, LOWER], ext.at[:, 1:3, TOP], below),
        ],
        "x": [link(outer, outer, ext.at[:, edge, MIDDLE], ext.at[:, far, MIDDLE], beside)],
        "i": [link(always, always, ext.at[:, inner, MIDDLE], ext.at[:, halo, MIDDLE], other)],
        "xy": [
            link(up & outer, down & outer, ext.at[:, halo, UPPER], ext.at[:, halo, BOTTOM], above),
            link(down & outer, up & outer, ext.at[:, halo, LOWER], ext.at[:, halo, TOP], below),
        ],
        "iy": [
            link(up, up, ext.at[:, inner, TOP], ext.at[:, halo, TOP], other),
            link(down, down, ext.at[:, inner, BOTTOM], ext.at[:, halo, BOTTOM], other),
        ],
    }


def inward(grad, box, corners, send, recv):
    core, up, down, outer = around()
    above, below, beside, other = devices_around()
    link = sides(send, recv)
    edge, inner = pl.ds(1 + core, 1), pl.ds(2 - core, 1)
    halo, far = pl.ds(3 * core, 1), pl.ds(3 - 3 * core, 1)
    always = up | jnp.logical_not(up)
    return {
        "xy": [
            link(up & outer, down & outer, grad.at[:, halo, TOP], corners.at[:, 0:1], above),
            link(down & outer, up & outer, grad.at[:, halo, BOTTOM], corners.at[:, 1:2], below),
        ],
        "iy": [
            link(up, up, grad.at[:, far, TOP], corners.at[:, 2:3], other),
            link(down, down, grad.at[:, far, BOTTOM], corners.at[:, 3:4], other),
        ],
        "y": [
            link(up, down, grad.at[:, edge, TOP], box.at[:, edge, TOP], above),
            link(down, up, grad.at[:, edge, BOTTOM], box.at[:, edge, BOTTOM], below),
        ],
        "z": [
            link(up, down, grad.at[:, inner, TOP], box.at[:, inner, TOP], above),
            link(down, up, grad.at[:, inner, BOTTOM], box.at[:, inner, BOTTOM], below),
        ],
        "i": [link(always, always, grad.at[:, far, MIDDLE], box.at[:, far, MIDDLE], other)],
        "x": [link(outer, outer, grad.at[:, halo, MIDDLE], box.at[:, halo, MIDDLE], beside)],
    }


def start_sides(copies):
    for ok, _, copy in copies:
        pl.when(ok)(copy.start)


def take_sides(copies):
    for _, arrives, copy in copies:
        pl.when(arrives)(copy.wait_recv)


def leave_sides(copies):
    for ok, _, copy in copies:
        pl.when(ok)(copy.wait_send)


def blank_outside(ext):
    gy, gx = lax.axis_index("gy"), lax.axis_index("gx")
    for outside, place in (
        (gy == 0, (slice(0, 4), TOP)),
        (gy == lax.axis_size("gy") - 1, (slice(0, 4), BOTTOM)),
        (gx == 0, (slice(0, 1), slice(0, 512))),
        (gx == lax.axis_size("gx") - 1, (slice(3, 4), slice(0, 512))),
    ):

        @pl.when(outside)
        def _(place=place):
            cols, rows = place
            ext[:, cols, rows, :] = jnp.zeros((2, cols.stop - cols.start, rows.stop - rows.start, 128), F32)


def arrange(amps, sort, out):
    def one(k, carry):
        half = jnp.dot(sort[0], amps[0, 0, k], preferred_element_type=F32).astype(BF16)
        out[k] = jnp.dot(half, sort[1], preferred_element_type=F32).astype(BF16)
        return carry

    lax.fori_loop(0, out.shape[0], one, jnp.int32(0))


def split(x):
    hi = x.astype(BF16)
    return hi, (x - hi.astype(F32)).astype(BF16)


def right_dot(hi, lo, m):
    return jnp.dot(
        jnp.concatenate([hi, lo, hi], axis=1),
        jnp.concatenate([m[0], m[0], m[1]], axis=0),
        preferred_element_type=F32,
    )


def left_dot(m, hi, lo):
    return jnp.dot(
        jnp.concatenate([m[0], m[0], m[1]], axis=1),
        jnp.concatenate([hi, lo, hi], axis=0),
        preferred_element_type=F32,
    )


def corner(positions, k):
    row = positions[0, 0, k, 0] - lax.axis_index("gy") * 256 + 128
    col = positions[0, 0, k, 1] - lax.axis_index("gx") * 256 + 128
    return jnp.clip(row, 0, 255), jnp.clip(col, 0, 255)


def cut_patches(positions, ext, cut, total):
    total[4:6] = jnp.zeros((2, 256, 128), F32)
    lane = lax.broadcasted_iota(jnp.int32, (1, 128), 1)

    def visit(k, carry):
        r, c = corner(positions, k)
        first = lax.div(c, 128)
        c = lax.rem(c, 128)
        back = lax.rem(128 - c, 128)
        keep = lane < 128 - c
        for i in range(0, 256, 64):
            rows = slice(i, i + 64)
            part = []
            for p in range(2):
                t = [pltpu.roll(ext[p, first + b, pl.ds(r + i, 64), :], back, 1) for b in range(3)]
                h = [jnp.where(keep, t[0], t[1]), jnp.where(keep, t[1], t[2])]
                for b in range(2):
                    cut[k, p, b, rows, :] = h[b]
                part.append(h)
            for b in range(2):
                total[4 + b, rows, :] += part[0][b] * part[0][b] + part[1][b] * part[1][b]
        return carry

    lax.fori_loop(0, cut.shape[0], visit, jnp.int32(0))


def gradients(positions, cut, probe, amps, right, left, total, lhs_hi, lhs_lo, chi, stage):
    total[0:4] = jnp.zeros((4, 256, 128), F32)
    chi[...] = jnp.zeros_like(chi)
    lane = lax.broadcasted_iota(jnp.int32, (1, 128), 1)
    pairs = cut.shape[0] // 2

    def waves(k, u):
        for i in range(0, 256, 64):
            rows = slice(i, i + 64)
            place = slice(256 * u + i, 256 * u + i + 64)
            wave = []
            for b in range(2):
                ore, oim = cut[k, 0, b, rows, :], cut[k, 1, b, rows, :]
                pre, pim = probe[0, b, rows, :], probe[1, b, rows, :]
                wave.append((pre * ore - pim * oim, pre * oim + pim * ore))
            for q in range(2):
                for p in range(2):
                    x = wave[0][p] + wave[1][p] if q == 0 else wave[0][p] - wave[1][p]
                    hi, lo = split(x)
                    lhs_hi[q, place, 128 * p : 128 * p + 128] = hi
                    lhs_lo[q, place, 128 * p : 128 * p + 128] = lo

    def correct(k, s, top, low):
        hi, lo = split(top + low if s == 0 else top - low)
        far = left_dot(left[s], hi, lo)
        re, im = far[:128], far[128:]
        factor = amps[k, 128 * s : 128 * s + 128, :].astype(F32) * lax.rsqrt(jnp.maximum(re * re + im * im, 0.25)) - 1.0
        hi, lo = split(jnp.concatenate([re * factor, im * factor], axis=0))
        return left_dot(right[s], hi, lo)

    def deposit(k, u):
        c = lax.rem(corner(positions, k)[1], 128)
        late = lane >= c
        for i in range(0, 256, 64):
            rows = slice(i, i + 64)
            place = slice(256 * u + i, 256 * u + i + 64)
            even, odd = chi[0, place, :], chi[1, place, :]
            g = [[], []]
            for b in range(2):
                x = even + odd if b == 0 else even - odd
                cre, cim = x[:, :128], x[:, 128:]
                pre, pim = probe[0, b, rows, :], probe[1, b, rows, :]
                ore, oim = cut[k, 0, b, rows, :], cut[k, 1, b, rows, :]
                total[b, rows, :] += ore * cre + oim * cim
                total[2 + b, rows, :] += ore * cim - oim * cre
                g[0].append(pltpu.roll(pre * cre + pim * cim, c, 1))
                g[1].append(pltpu.roll(pre * cim - pim * cre, c, 1))
            for p in range(2):
                to = pl.ds(pl.multiple_of(512 * k + 256 + i, 64), 64)
                stage[p, 1, to, :] = jnp.where(late, g[p][0], 0.0)
                stage[p, 2, to, :] = jnp.where(late, g[p][1], g[p][0])
                stage[p, 3, to, :] = jnp.where(late, 0.0, g[p][1])

    def stack(y, u):
        out = []
        for h in range(2):
            rows = slice(256 * u + 128 * h, 256 * u + 128 * h + 128)
            parts = [
                jnp.concatenate([y[0][rows, lanes], y[1][rows, lanes]], axis=1)
                for lanes in (slice(0, 128), slice(128, 256))
            ]
            out.append(jnp.concatenate(parts, axis=0))
        return out

    def visit(j, carry):
        y = [right_dot(lhs_hi[q], lhs_lo[q], right[q]) for q in range(2)]
        for u in range(2):
            deposit(2 * jnp.maximum(j - 1, 0) + u, u)
        half = [[], []]
        for s in range(2):
            for u in range(2):
                top, low = stack(y, u)
                half[u].append(correct(2 * j + u, s, top, low))
        for q in range(2):
            lanes = slice(128 * q, 128 * q + 128)
            parts = []
            for u in range(2):
                for x in (half[u][0] + half[u][1], half[u][0] - half[u][1]):
                    parts.append(jnp.concatenate([x[:128, lanes], x[128:, lanes]], axis=1))
            hi, lo = split(jnp.concatenate(parts, axis=0))
            chi[q] = right_dot(hi, lo, left[q])
        for u in range(2):
            waves(2 * jnp.minimum(j + 1, pairs - 1) + u, u)
        return carry

    for u in range(2):
        waves(u, u)
    lax.fori_loop(0, pairs, visit, jnp.int32(0))
    for u in range(2):
        deposit(2 * pairs - 2 + u, u)


def gather(positions, stage, grad, cols, rows):
    def part(i, carry):
        start = pl.multiple_of(i * 64, 64)
        for p in range(2):
            for b in cols:
                x = jnp.zeros((64, 128), F32)
                for k in range(stage.shape[2] // 512):
                    r, c = corner(positions, k)
                    x = x + stage[p, lax.rem(b + 1 - lax.div(c, 128), 4), pl.ds(512 * k + 256 + start - r, 64), :]
                grad[p, b, pl.ds(start, 64), :] = x
        return carry

    lax.fori_loop(rows.start // 64, rows.stop // 64, part, jnp.int32(0))


def sibling():
    gy, gx = lax.axis_index("gy"), lax.axis_index("gx")
    return gy, gx + 1 - 2 * lax.rem(gx, 2)


def along_x(d):
    gy, gx = lax.axis_index("gy"), lax.axis_index("gx")
    x = lax.div(gx, 4)
    return gy, lax.rem(x + d, 4) * 4 + lax.rem(gx, 4)


def member(j):
    gx = lax.axis_index("gx")
    place = lax.rem(j, 8)
    return lax.div(j, 8) * 4 + lax.div(place, 2), lax.div(gx, 4) * 4 + lax.rem(place, 2) * 2 + lax.rem(gx, 2)


class Sum:
    def __init__(self, total, full, acc0, acc1, acc2, rb0, rb1, rb2, send, recv):
        self.total, self.full, self.acc0, self.acc1, self.acc2 = total, full, acc0, acc1, acc2
        self.rb0, self.rb1, self.rb2 = rb0, rb1, rb2
        self.send, self.recv = send, recv
        gy, gx = lax.axis_index("gy"), lax.axis_index("gx")
        self.core, self.x = lax.rem(gx, 2), lax.div(gx, 4)
        self.mine = lax.rem(gy, 4) * 2 + lax.div(lax.rem(gx, 4), 2)
        self.me = lax.div(gy, 4) * 8 + self.mine
        self.tiles = total.shape[0] // 2

    def greet(self, barrier):
        devices = [sibling()] + [along_x(d) for d in (1, 2, 3)] + [member(lax.rem(self.me + d, 16)) for d in range(1, 16)]
        for device in devices:
            pl.semaphore_signal(barrier, inc=1, device_id=device, device_id_type=MESH)
        return len(devices)

    def copy(self, source, target, i, device):
        return pltpu.make_async_remote_copy(
            source, target, self.send.at[i], self.recv.at[i], device_id=device, device_id_type=MESH
        )

    def copies0(self):
        theirs = pl.ds(pl.multiple_of((1 - self.core) * 128, 128), 128)
        return [self.copy(self.total.at[:, theirs, :], self.rb0, 0, sibling())]

    def copies1(self):
        out = []
        for d in (1, 2, 3):
            part = pl.ds(pl.multiple_of(lax.rem(self.x + d, 4) * 32, 32), 32)
            out.append(self.copy(self.acc0.at[:, part, :], self.rb1.at[d - 1], d, along_x(d)))
        return out

    def copies2(self):
        out = []
        for d in range(1, 16):
            to = lax.rem(self.me + d, 16)
            part = pl.ds(lax.rem(to, 8) * self.tiles, self.tiles)
            out.append(self.copy(self.acc1.at[part], self.rb2.at[self.me], 3 + d, member(to)))
        return out

    def copies3(self):
        place = self.full.at[self.core, self.x, pl.ds(self.mine * self.tiles, self.tiles)]
        out = []
        for d in range(1, 8):
            to = lax.rem(self.mine + d, 8) + lax.div(self.me, 8) * 8
            out.append(self.copy(self.acc2, place, 18 + d, member(to)))
        return out

    def copies4(self):
        place = self.full.at[self.core, self.x]
        return [self.copy(place, place, 25 + d, along_x(d)) for d in (1, 2, 3)]

    def copies5(self):
        place = self.full.at[self.core]
        return [self.copy(place, place, 29, sibling())]

    def step(self, number):
        if number > 0:
            for c in getattr(self, f"copies{number - 1}")():
                c.wait_recv()
        if number == 1:
            own = pl.ds(pl.multiple_of(self.core * 128, 128), 128)
            self.acc0[...] = self.total[:, own, :] + self.rb0[...]
        if number == 2:
            own = pl.ds(pl.multiple_of(self.x * 32, 32), 32)
            x = self.acc0[:, own, :] + self.rb1[0] + self.rb1[1] + self.rb1[2]
            self.acc1[...] = x.reshape(self.acc1.shape)
            self.rb2[pl.ds(self.me, 1)] = self.acc1[pl.ds(self.mine * self.tiles, self.tiles)][None]
        if number == 3:
            x = self.rb2[0]
            for j in range(1, 16):
                x = x + self.rb2[j]
            self.acc2[...] = x
            self.full[pl.ds(self.core, 1), pl.ds(self.x, 1), pl.ds(self.mine * self.tiles, self.tiles)] = x[None, None]
        if number < 6:
            for c in getattr(self, f"copies{number}")():
                c.start()
        else:
            for stage in range(6):
                for c in getattr(self, f"copies{stage}")():
                    c.wait_send()


def sum_scratch(n):
    return [
        pltpu.VMEM((2, 4, 4 * n, 8, 128), F32),
        pltpu.VMEM((n, 128, 128), F32),
        pltpu.VMEM((4 * n, 8, 128), F32),
        pltpu.VMEM((n // 2, 8, 128), F32),
        pltpu.VMEM((n, 128, 128), F32),
        pltpu.VMEM((3, n, 32, 128), F32),
        pltpu.VMEM((16, n // 2, 8, 128), F32),
        pltpu.SemaphoreType.DMA((30,)),
        pltpu.SemaphoreType.DMA((30,)),
    ]


def new_probe(probe, full, write):
    parts = [full[h, x, 16:24] for h in range(2) for x in range(4)]
    top = parts[0]
    for w in parts[1:]:
        top = jnp.maximum(top, w)
    floor = 0.1 * jnp.max(top)
    for h in range(2):
        for x in range(4):
            rows = slice(128 * h + 32 * x, 128 * h + 32 * x + 32)
            for b in range(2):
                w = 0.9 * full[h, x, 16 + 4 * b : 20 + 4 * b].reshape(32, 128) + floor
                for p in range(2):
                    g = full[h, x, 8 * p + 4 * b : 8 * p + 4 * b + 4].reshape(32, 128)
                    write(p, b, rows, probe[p, b, rows, :] + g / w)


ORDERS = (
    ("s0", "gh", "b0", "s1", "go", "b1", "b2", "s2", "s3", "s4", "w", "u", "c0", "s5", "c1", "c2", "s6", "p", "cw"),
    ("s0", "gh", "b0", "s1", "go", "b1", "s2", "b2", "s3", "s4", "w", "u", "s5", "s6", "p"),
)


def kernel(positions, obj, probe, amps, right, left, sort, obj_out, probe_out, *refs):
    ext, grad, total, acc, probes, arranged, cut, lhs_hi, lhs_lo, chi, stage, inbox, corners, send, recv, *rest = refs
    size = len(rest) // 2
    sums = [Sum(total, *rest[size * step : size * (step + 1)]) for step in range(2)]
    for step in range(2):
        blank_outside(ext.at[step])
    barrier, count = greet_sides()
    count = count + sums[0].greet(barrier)
    for b in range(2):
        lanes = slice(128 * b, 128 * b + 128)
        ext[0, :, 1 + b, 128:384, :] = obj[:, :, lanes]
        probes[0, :, b] = probe[:, :, lanes]

    def clear(k, carry):
        for p in range(2):
            for b in range(4):
                stage[p, b, pl.ds(pl.multiple_of(512 * k, 512), 256), :] = jnp.zeros((256, 128), F32)
            stage[p, 0, pl.ds(pl.multiple_of(512 * k + 256, 256), 256), :] = jnp.zeros((256, 128), F32)
        return carry

    lax.fori_loop(0, cut.shape[0], clear, jnp.int32(0))
    stage[:, :, 512 * cut.shape[0] :, :] = jnp.zeros((2, 4, 256, 128), F32)
    pl.semaphore_wait(barrier, count)
    copies = outward(ext.at[0], send.at[0], recv.at[0])
    start_sides(copies["x"] + copies["y"] + copies["i"])
    take_sides(copies["x"])
    start_sides(copies["xy"])
    arrange(amps, sort, arranged)
    take_sides(copies["y"])
    start_sides(copies["iy"])
    take_sides(copies["xy"] + copies["i"] + copies["iy"])
    leave_sides(sum(copies.values(), []))
    for step in range(2):
        old, now = ext.at[step], probes.at[step]
        cut_patches(positions, old, cut, total)
        gradients(positions, cut, now, arranged, right, left, total, lhs_hi, lhs_lo, chi, stage)
        update(step, positions, stage, grad, inbox.at[step], corners.at[step], acc, old, ext.at[1], now, probes.at[1], sums[step], send, recv, obj_out, probe_out)


def update(step, positions, stage, grad, inbox, corners, acc, old, new, now, later, adder, send, recv, obj_out, probe_out):
    peak = jnp.max(now[0] * now[0] + now[1] * now[1])
    into = inward(grad, inbox, corners, send.at[1 + 2 * step], recv.at[1 + 2 * step])
    out = outward(new, send.at[2], recv.at[2]) if step == 0 else None
    core, up, down, outer = around()
    gx = lax.axis_index("gx")
    inner, halo = pl.ds(2 - core, 1), pl.ds(3 * core, 1)

    def add(where, target, place, value):
        @pl.when(where)
        def _():
            target[place] += value()

    def write(p, b, rows, x):
        if step == 1:
            probe_out[p, rows, 128 * b : 128 * b + 128] = x
        else:
            later[p, b, rows, :] = x

    for event in ORDERS[step]:
        if event == "gh":
            gather(positions, stage, grad, range(4), TOP)
            gather(positions, stage, grad, range(4), BOTTOM)
            gather(positions, stage, grad, (0, 3), MIDDLE)
        elif event == "go":
            gather(positions, stage, grad, (1, 2), MIDDLE)
            acc[...] = grad[:, 1:3, MIDDLE, :]
        elif event == "b0":
            start_sides(into["iy"] + into["xy"] + into["y"] + into["i"])
        elif event == "b1":
            take_sides(into["iy"])
            add(up, grad, (slice(None), inner, TOP), lambda: corners[:, 2:3])
            add(down, grad, (slice(None), inner, BOTTOM), lambda: corners[:, 3:4])
            start_sides(into["z"])
        elif event == "b2":
            take_sides(into["xy"])
            add(down & outer, grad, (slice(None), halo, LOWER), lambda: corners[:, 0:1])
            add(up & outer, grad, (slice(None), halo, UPPER), lambda: corners[:, 1:2])
            start_sides(into["x"])
        elif event == "w":
            take_sides(into["y"] + into["z"] + into["i"] + into["x"])
            leave_sides(sum(into.values(), []))
            every = slice(None)
            add(down, acc, (every, every, slice(128, 256)), lambda: inbox[:, 1:3, TOP])
            add(up, acc, (every, every, slice(0, 128)), lambda: inbox[:, 1:3, BOTTOM])
            add(gx > 0, acc, (every, 0), lambda: inbox[:, 3, MIDDLE])
            add(gx < lax.axis_size("gx") - 1, acc, (every, 1), lambda: inbox[:, 0, MIDDLE])
        elif event == "c0":
            start_sides(out["x"] + out["y"] + out["i"])
        elif event == "c1":
            take_sides(out["x"])
            start_sides(out["xy"])
        elif event == "c2":
            take_sides(out["y"])
            start_sides(out["iy"])
        elif event == "cw":
            take_sides(out["xy"] + out["i"] + out["iy"])
            leave_sides(sum(out.values(), []))
        elif event[0] == "s":
            adder.step(int(event[1]))
        elif event == "u" and step == 1:
            for b in range(2):
                obj_out[:, :, 128 * b : 128 * b + 128] = old[:, 1 + b, 128:384, :] + acc[:, b] / peak
        elif event == "u":
            new[:, 1:3, 128:384, :] = old[:, 1:3, 128:384, :] + acc[...] / peak
        else:
            new_probe(now, adder.full, write)


def shards(obj, probe, positions, amps):
    count = positions.shape[2]
    right, left = (jnp.asarray(t) for t in tables())
    tile = jax.ShapeDtypeStruct((2, 256, 256), F32)
    ext = (2, 4, 512, 128)
    return pl.pallas_call(
        kernel,
        out_shape=(tile, tile),
        in_specs=[SMEM] + [VMEM] * 6,
        out_specs=(VMEM, VMEM),
        scratch_shapes=[
            pltpu.VMEM((2, *ext), F32),
            pltpu.VMEM(ext, F32),
            pltpu.VMEM((6, 256, 128), F32),
            pltpu.VMEM((2, 2, 256, 128), F32),
            pltpu.VMEM((2, 2, 2, 256, 128), F32),
            pltpu.VMEM((count, 256, 256), BF16),
            pltpu.VMEM((count, 2, 2, 256, 128), F32),
            pltpu.VMEM((2, 512, 256), BF16),
            pltpu.VMEM((2, 512, 256), BF16),
            pltpu.VMEM((2, 512, 256), F32),
            pltpu.VMEM((2, 4, 512 * count + 256, 128), F32),
            pltpu.VMEM((2, *ext), F32),
            pltpu.VMEM((2, 2, 4, 128, 128), F32),
            pltpu.SemaphoreType.DMA((4, 16)),
            pltpu.SemaphoreType.DMA((4, 16)),
            *sum_scratch(6) * 2,
        ],
        compiler_params=pltpu.CompilerParams(collective_id=0, has_side_effects=True, vmem_limit_bytes=VMEM_LIMIT),
        name="iterations",
    )(positions, obj, probe, amps, right, left, jnp.asarray(sorting()))


def solution(mesh):
    in_specs = (
        P(None, "gy", "gx"),
        P(),
        P("gy", "gx", None, None),
        P("gy", "gx", None, None, None),
    )
    out_specs = (P(None, "gy", "gx"), P())
    return jax.shard_map(shards, mesh=mesh, in_specs=in_specs, out_specs=out_specs, check_vma=False)
```

```python
import functools

import jax
import jax.numpy as jnp
import ml_dtypes
import numpy as np
from jax import lax
from jax.experimental import pallas as pl
from jax.experimental.pallas import tpu as pltpu
from jax.sharding import PartitionSpec as P

MESH = pl.DeviceIdType.MESH
F32 = jnp.float32
BF16 = jnp.bfloat16
VMEM = pl.BlockSpec(memory_space=pltpu.VMEM)
SMEM = pl.BlockSpec(memory_space=pltpu.SMEM)
VMEM_LIMIT = 60 * 1024 * 1024

TOP, UPPER, LOWER, BOTTOM = (slice(128 * i, 128 * i + 128) for i in range(4))
MIDDLE = slice(128, 384)


def tables():
    n = np.arange(128)[:, None]
    out = []
    for parity in range(2):
        turns = (n * (2 * np.arange(128)[None, :] + parity)) % 256
        angle = -2.0 * np.pi * turns / 256.0
        re, im = np.cos(angle) / 16.0, np.sin(angle) / 16.0
        m = np.block([[re, im], [-im, re]]).astype(np.float32)
        hi = m.astype(ml_dtypes.bfloat16)
        lo = (m - hi.astype(np.float32)).astype(ml_dtypes.bfloat16)
        out.append(np.stack([hi, lo]))
    right = np.stack(out)
    return right, np.ascontiguousarray(np.swapaxes(right, 2, 3))


def sorting():
    m = np.zeros((256, 256), np.float32)
    m[np.arange(256), np.concatenate([np.arange(0, 256, 2), np.arange(1, 256, 2)])] = 1.0
    return np.stack([m, m.T]).astype(ml_dtypes.bfloat16)


def around():
    gy, gx = lax.axis_index("gy"), lax.axis_index("gx")
    core = lax.rem(gx, 2)
    outer = jnp.where(core == 0, gx > 0, gx < lax.axis_size("gx") - 1)
    return core, gy > 0, gy < lax.axis_size("gy") - 1, outer


def devices_around():
    gy, gx = lax.axis_index("gy"), lax.axis_index("gx")
    core = lax.rem(gx, 2)
    ny, nx = lax.axis_size("gy"), lax.axis_size("gx")
    return (
        (jnp.maximum(gy - 1, 0), gx),
        (jnp.minimum(gy + 1, ny - 1), gx),
        (gy, jnp.clip(gx + 2 * core - 1, 0, nx - 1)),
        (gy, gx + 1 - 2 * core),
    )


def greet_sides():
    barrier = pltpu.get_barrier_semaphore()
    count = jnp.int32(0)
    for ok, device in zip(around()[1:], devices_around()):

        @pl.when(ok)
        def _(device=device):
            pl.semaphore_signal(barrier, inc=1, device_id=device, device_id_type=MESH)

        count = count + ok.astype(jnp.int32)
    return barrier, count


def sides(send, recv):
    slots = iter(range(16))

    def link(goes, comes, source, target, device):
        i = next(slots)
        return (
            goes,
            comes,
            pltpu.make_async_remote_copy(
                source, target, send.at[i], recv.at[i], device_id=device, device_id_type=MESH
            ),
        )

    return link


def outward(ext, send, recv):
    core, up, down, outer = around()
    above, below, beside, other = devices_around()
    link = sides(send, recv)
    edge, inner = pl.ds(1 + core, 1), pl.ds(2 - core, 1)
    halo, far = pl.ds(3 * core, 1), pl.ds(3 - 3 * core, 1)
    always = up | jnp.logical_not(up)
    return {
        "y": [
            link(up, down, ext.at[:, 1:3, UPPER], ext.at[:, 1:3, BOTTOM], above),
            link(down, up, ext.at[:, 1:3, LOWER], ext.at[:, 1:3, TOP], below),
        ],
        "x": [link(outer, outer, ext.at[:, edge, MIDDLE], ext.at[:, far, MIDDLE], beside)],
        "i": [link(always, always, ext.at[:, inner, MIDDLE], ext.at[:, halo, MIDDLE], other)],
        "xy": [
            link(up & outer, down & outer, ext.at[:, halo, UPPER], ext.at[:, halo, BOTTOM], above),
            link(down & outer, up & outer, ext.at[:, halo, LOWER], ext.at[:, halo, TOP], below),
        ],
        "iy": [
            link(up, up, ext.at[:, inner, TOP], ext.at[:, halo, TOP], other),
            link(down, down, ext.at[:, inner, BOTTOM], ext.at[:, halo, BOTTOM], other),
        ],
    }


def inward(grad, box, corners, send, recv):
    core, up, down, outer = around()
    above, below, beside, other = devices_around()
    link = sides(send, recv)
    edge, inner = pl.ds(1 + core, 1), pl.ds(2 - core, 1)
    halo, far = pl.ds(3 * core, 1), pl.ds(3 - 3 * core, 1)
    always = up | jnp.logical_not(up)
    return {
        "xy": [
            link(up & outer, down & outer, grad.at[:, halo, TOP], corners.at[:, 0:1], above),
            link(down & outer, up & outer, grad.at[:, halo, BOTTOM], corners.at[:, 1:2], below),
        ],
        "iy": [
            link(up, up, grad.at[:, far, TOP], corners.at[:, 2:3], other),
            link(down, down, grad.at[:, far, BOTTOM], corners.at[:, 3:4], other),
        ],
        "y": [
            link(up, down, grad.at[:, edge, TOP], box.at[:, edge, TOP], above),
            link(down, up, grad.at[:, edge, BOTTOM], box.at[:, edge, BOTTOM], below),
        ],
        "z": [
            link(up, down, grad.at[:, inner, TOP], box.at[:, inner, TOP], above),
            link(down, up, grad.at[:, inner, BOTTOM], box.at[:, inner, BOTTOM], below),
        ],
        "i": [link(always, always, grad.at[:, far, MIDDLE], box.at[:, far, MIDDLE], other)],
        "x": [link(outer, outer, grad.at[:, halo, MIDDLE], box.at[:, halo, MIDDLE], beside)],
    }


def start_sides(copies):
    for ok, _, copy in copies:
        pl.when(ok)(copy.start)


def take_sides(copies):
    for _, arrives, copy in copies:
        pl.when(arrives)(copy.wait_recv)


def leave_sides(copies):
    for ok, _, copy in copies:
        pl.when(ok)(copy.wait_send)


def blank_outside(ext):
    gy, gx = lax.axis_index("gy"), lax.axis_index("gx")
    for outside, place in (
        (gy == 0, (slice(0, 4), TOP)),
        (gy == lax.axis_size("gy") - 1, (slice(0, 4), BOTTOM)),
        (gx == 0, (slice(0, 1), slice(0, 512))),
        (gx == lax.axis_size("gx") - 1, (slice(3, 4), slice(0, 512))),
    ):

        @pl.when(outside)
        def _(place=place):
            cols, rows = place
            ext[:, cols, rows, :] = jnp.zeros((2, cols.stop - cols.start, rows.stop - rows.start, 128), F32)


def arrange(amps, sort, out):
    def one(k, carry):
        half = jnp.dot(sort[0], amps[k], preferred_element_type=F32).astype(BF16)
        out[k] = jnp.dot(half, sort[1], preferred_element_type=F32).astype(BF16)
        return carry

    lax.fori_loop(0, out.shape[0], one, jnp.int32(0))


def split(x):
    hi = x.astype(BF16)
    return hi, (x - hi.astype(F32)).astype(BF16)


def right_dot(hi, lo, m):
    return jnp.dot(
        jnp.concatenate([hi, lo, hi], axis=1),
        jnp.concatenate([m[0], m[0], m[1]], axis=0),
        preferred_element_type=F32,
    )


def left_dot(m, hi, lo):
    first = jnp.dot(jnp.concatenate([m[0], m[1]], axis=0), hi, preferred_element_type=F32)
    return first[:256] + (first[256:] + jnp.dot(m[0], lo, preferred_element_type=F32))


def corner(positions, k):
    row = positions[0, 0, k, 0] - lax.axis_index("gy") * 256 + 128
    col = positions[0, 0, k, 1] - lax.axis_index("gx") * 256 + 128
    return jnp.clip(row, 0, 255), jnp.clip(col, 0, 255)


def cut_patches(positions, ext, cut, total):
    total[4:6] = jnp.zeros((2, 256, 128), F32)
    lane = lax.broadcasted_iota(jnp.int32, (1, 128), 1)

    def visit(k, carry):
        r, c = corner(positions, k)
        first = lax.div(c, 128)
        c = lax.rem(c, 128)
        back = lax.rem(128 - c, 128)
        keep = lane < 128 - c
        for i in range(0, 256, 64):
            rows = slice(i, i + 64)
            part = []
            for p in range(2):
                t = [pltpu.roll(ext[p, first + b, pl.ds(r + i, 64), :], back, 1) for b in range(3)]
                h = [jnp.where(keep, t[0], t[1]), jnp.where(keep, t[1], t[2])]
                for b in range(2):
                    cut[k, p, b, rows, :] = h[b]
                part.append(h)
            for b in range(2):
                total[4 + b, rows, :] += part[0][b] * part[0][b] + part[1][b] * part[1][b]
        return carry

    lax.fori_loop(0, cut.shape[0], visit, jnp.int32(0))


def gradients(positions, cut, probe, amps, right, left, total, lhs_hi, lhs_lo, chi, stage, heavy):
    total[0:4] = jnp.zeros((4, 256, 128), F32)
    chi[...] = jnp.zeros_like(chi)
    lane = lax.broadcasted_iota(jnp.int32, (1, 128), 1)
    pairs = cut.shape[0] // 2

    def waves(k, u):
        for i in range(0, 256, 64):
            rows = slice(i, i + 64)
            place = slice(256 * u + i, 256 * u + i + 64)
            wave = []
            for b in range(2):
                ore, oim = cut[k, 0, b, rows, :], cut[k, 1, b, rows, :]
                pre, pim = probe[0, b, rows, :], probe[1, b, rows, :]
                wave.append((pre * ore - pim * oim, pre * oim + pim * ore))
            for q in range(2):
                for p in range(2):
                    x = wave[0][p] + wave[1][p] if q == 0 else wave[0][p] - wave[1][p]
                    hi, lo = split(x)
                    lhs_hi[q, place, 128 * p : 128 * p + 128] = hi
                    lhs_lo[q, place, 128 * p : 128 * p + 128] = lo

    def correct(k, s, top, low):
        hi, lo = split(top + low if s == 0 else top - low)
        far = left_dot(left[s], hi, lo)
        re, im = far[:128], far[128:]
        factor = amps[k, 128 * s : 128 * s + 128, :].astype(F32) * lax.rsqrt(jnp.maximum(re * re + im * im, 0.25)) - 1.0
        hi, lo = split(jnp.concatenate([re * factor, im * factor], axis=0))
        return left_dot(right[s], hi, lo)

    def deposit(k, u):
        c = lax.rem(corner(positions, k)[1], 128)
        late = lane >= c
        for i in range(0, 256, 64):
            rows = slice(i, i + 64)
            place = slice(256 * u + i, 256 * u + i + 64)
            even, odd = chi[0, place, :], chi[1, place, :]
            g = [[], []]
            for b in range(2):
                x = even + odd if b == 0 else even - odd
                cre, cim = x[:, :128], x[:, 128:]
                pre, pim = probe[0, b, rows, :], probe[1, b, rows, :]
                ore, oim = cut[k, 0, b, rows, :], cut[k, 1, b, rows, :]
                total[b, rows, :] += ore * cre + oim * cim
                total[2 + b, rows, :] += ore * cim - oim * cre
                g[0].append(pltpu.roll(pre * cre + pim * cim, c, 1))
                g[1].append(pltpu.roll(pre * cim - pim * cre, c, 1))
            for p in range(2):
                to = pl.ds(pl.multiple_of(512 * k + 256 + i, 64), 64)
                stage[p, 1, to, :] = jnp.where(late, g[p][0], 0.0)
                stage[p, 2, to, :] = jnp.where(late, g[p][1], g[p][0])
                stage[p, 3, to, :] = jnp.where(late, 0.0, g[p][1])

    def stack(y, u):
        out = []
        for h in range(2):
            rows = slice(256 * u + 128 * h, 256 * u + 128 * h + 128)
            parts = [
                jnp.concatenate([y[0][rows, lanes], y[1][rows, lanes]], axis=1)
                for lanes in (slice(0, 128), slice(128, 256))
            ]
            out.append(jnp.concatenate(parts, axis=0))
        return out

    def visit(j, carry):
        pl.when(j == 1)(functools.partial(heavy.step, 1))
        pl.when(j == pairs - 1)(functools.partial(heavy.step, 2))
        y = [right_dot(lhs_hi[q], lhs_lo[q], right[q]) for q in range(2)]
        for u in range(2):
            deposit(2 * jnp.maximum(j - 1, 0) + u, u)
        half = [[], []]
        for s in range(2):
            for u in range(2):
                top, low = stack(y, u)
                half[u].append(correct(2 * j + u, s, top, low))
        for q in range(2):
            lanes = slice(128 * q, 128 * q + 128)
            parts = []
            for u in range(2):
                for x in (half[u][0] + half[u][1], half[u][0] - half[u][1]):
                    parts.append(jnp.concatenate([x[:128, lanes], x[128:, lanes]], axis=1))
            hi, lo = split(jnp.concatenate(parts, axis=0))
            chi[q] = right_dot(hi, lo, left[q])
        for u in range(2):
            waves(2 * jnp.minimum(j + 1, pairs - 1) + u, u)
        return carry

    for u in range(2):
        waves(u, u)
    lax.fori_loop(0, pairs, visit, jnp.int32(0))
    for u in range(2):
        deposit(2 * pairs - 2 + u, u)


def gather(positions, stage, grad, cols, rows):
    def part(i, carry):
        start = pl.multiple_of(i * 64, 64)
        for p in range(2):
            for b in cols:
                x = jnp.zeros((64, 128), F32)
                for k in range(stage.shape[2] // 512):
                    r, c = corner(positions, k)
                    x = x + stage[p, lax.rem(b + 1 - lax.div(c, 128), 4), pl.ds(512 * k + 256 + start - r, 64), :]
                grad[p, b, pl.ds(start, 64), :] = x
        return carry

    lax.fori_loop(rows.start // 64, rows.stop // 64, part, jnp.int32(0))


def sibling():
    gy, gx = lax.axis_index("gy"), lax.axis_index("gx")
    return gy, gx + 1 - 2 * lax.rem(gx, 2)


def along_x(d):
    gy, gx = lax.axis_index("gy"), lax.axis_index("gx")
    x = lax.div(gx, 4)
    return gy, lax.rem(x + d, 4) * 4 + lax.rem(gx, 4)


def member(j):
    gx = lax.axis_index("gx")
    place = lax.rem(j, 8)
    return lax.div(j, 8) * 4 + lax.div(place, 2), lax.div(gx, 4) * 4 + lax.rem(place, 2) * 2 + lax.rem(gx, 2)


class Sum:
    def __init__(self, total, full, acc0, acc1, acc2, rb0, rb1, rb2, send, recv):
        self.total, self.full, self.acc0, self.acc1, self.acc2 = total, full, acc0, acc1, acc2
        self.rb0, self.rb1, self.rb2 = rb0, rb1, rb2
        self.send, self.recv = send, recv
        gy, gx = lax.axis_index("gy"), lax.axis_index("gx")
        self.core, self.x = lax.rem(gx, 2), lax.div(gx, 4)
        self.mine = lax.rem(gy, 4) * 2 + lax.div(lax.rem(gx, 4), 2)
        self.me = lax.div(gy, 4) * 8 + self.mine
        self.tiles = total.shape[0] // 2

    def greet(self, barrier):
        devices = [sibling()] + [along_x(d) for d in (1, 2, 3)] + [member(lax.rem(self.me + d, 16)) for d in range(1, 16)]
        for device in devices:
            pl.semaphore_signal(barrier, inc=1, device_id=device, device_id_type=MESH)
        return len(devices)

    def copy(self, source, target, i, device):
        return pltpu.make_async_remote_copy(
            source, target, self.send.at[i], self.recv.at[i], device_id=device, device_id_type=MESH
        )

    def copies0(self):
        theirs = pl.ds(pl.multiple_of((1 - self.core) * 128, 128), 128)
        return [self.copy(self.total.at[:, theirs, :], self.rb0, 0, sibling())]

    def copies1(self):
        out = []
        for d in (1, 2, 3):
            part = pl.ds(pl.multiple_of(lax.rem(self.x + d, 4) * 32, 32), 32)
            out.append(self.copy(self.acc0.at[:, part, :], self.rb1.at[d - 1], d, along_x(d)))
        return out

    def copies2(self):
        out = []
        for d in range(1, 16):
            to = lax.rem(self.me + d, 16)
            part = pl.ds(lax.rem(to, 8) * self.tiles, self.tiles)
            out.append(self.copy(self.acc1.at[part], self.rb2.at[self.me], 3 + d, member(to)))
        return out

    def copies3(self):
        place = self.full.at[self.core, self.x, pl.ds(self.mine * self.tiles, self.tiles)]
        out = []
        for d in range(1, 8):
            to = lax.rem(self.mine + d, 8) + lax.div(self.me, 8) * 8
            out.append(self.copy(self.acc2, place, 18 + d, member(to)))
        return out

    def copies4(self):
        place = self.full.at[self.core, self.x]
        return [self.copy(place, place, 25 + d, along_x(d)) for d in (1, 2, 3)]

    def copies5(self):
        place = self.full.at[self.core]
        return [self.copy(place, place, 29, sibling())]

    def step(self, number):
        if number > 0:
            for c in getattr(self, f"copies{number - 1}")():
                c.wait_recv()
        if number == 1:
            own = pl.ds(pl.multiple_of(self.core * 128, 128), 128)
            self.acc0[...] = self.total[:, own, :] + self.rb0[...]
        if number == 2:
            own = pl.ds(pl.multiple_of(self.x * 32, 32), 32)
            x = self.acc0[:, own, :] + self.rb1[0] + self.rb1[1] + self.rb1[2]
            self.acc1[...] = x.reshape(self.acc1.shape)
            self.rb2[pl.ds(self.me, 1)] = self.acc1[pl.ds(self.mine * self.tiles, self.tiles)][None]
        if number == 3:
            x = self.rb2[0]
            for j in range(1, 16):
                x = x + self.rb2[j]
            self.acc2[...] = x
            self.full[pl.ds(self.core, 1), pl.ds(self.x, 1), pl.ds(self.mine * self.tiles, self.tiles)] = x[None, None]
        if number < 6:
            for c in getattr(self, f"copies{number}")():
                c.start()
        else:
            for stage in range(6):
                for c in getattr(self, f"copies{stage}")():
                    c.wait_send()


def sum_scratch(n):
    return [
        pltpu.VMEM((2, 4, 4 * n, 8, 128), F32),
        pltpu.VMEM((n, 128, 128), F32),
        pltpu.VMEM((4 * n, 8, 128), F32),
        pltpu.VMEM((n // 2, 8, 128), F32),
        pltpu.VMEM((n, 128, 128), F32),
        pltpu.VMEM((3, n, 32, 128), F32),
        pltpu.VMEM((16, n // 2, 8, 128), F32),
        pltpu.SemaphoreType.DMA((30,)),
        pltpu.SemaphoreType.DMA((30,)),
    ]


def new_probe(probe, full, weight, write):
    parts = [weight[h, x] for h in range(2) for x in range(4)]
    top = parts[0]
    for w in parts[1:]:
        top = jnp.maximum(top, w)
    floor = 0.1 * jnp.max(top)
    for h in range(2):
        for x in range(4):
            rows = slice(128 * h + 32 * x, 128 * h + 32 * x + 32)
            for b in range(2):
                w = 0.9 * weight[h, x, 4 * b : 4 * b + 4].reshape(32, 128) + floor
                for p in range(2):
                    g = full[h, x, 8 * p + 4 * b : 8 * p + 4 * b + 4].reshape(32, 128)
                    write(p, b, rows, probe[p, b, rows, :] + g / w)


ORDERS = (
    ("s0", "g0", "s1", "g1", "g2", "t3", "go", "b1", "b2", "s2", "t4", "s3", "s4", "t5", "w", "u", "c0", "s5", "c1", "c2", "s6", "t6", "p", "cw"),
    ("s0", "g0", "s1", "g1", "g2", "t3", "go", "s2", "b1", "b2", "t4", "s3", "t5", "s4", "w", "u", "s5", "s6", "t6", "p"),
)


def kernel(positions, obj, probe, amps_far, right_far, left_far, sort_far, obj_out, probe_out, *refs):
    amps, right, left, sort, load, ext, grad, total, acc, probes, arranged, cut, lhs_hi, lhs_lo, chi, stage, inbox, corners, send, recv, *rest = refs
    size = len(rest) // 4
    parts = [rest[size * i : size * (i + 1)] for i in range(4)]
    sums = [Sum(total.at[0:4], *parts[step]) for step in range(2)]
    weights = [Sum(total.at[4:6], *parts[2 + step]) for step in range(2)]
    loads = [
        pltpu.make_async_copy(source, target, load.at[i])
        for i, (source, target) in enumerate(
            ((amps_far.at[0, 0], amps), (sort_far, sort), (right_far, right), (left_far, left))
        )
    ]
    for c in loads:
        c.start()
    for step in range(2):
        blank_outside(ext.at[step])
    barrier, count = greet_sides()
    count = count + sums[0].greet(barrier)
    for b in range(2):
        lanes = slice(128 * b, 128 * b + 128)
        ext[0, :, 1 + b, 128:384, :] = obj[:, :, lanes]
        probes[0, :, b] = probe[:, :, lanes]

    def clear(k, carry):
        for p in range(2):
            for b in range(4):
                stage[p, b, pl.ds(pl.multiple_of(512 * k, 512), 256), :] = jnp.zeros((256, 128), F32)
            stage[p, 0, pl.ds(pl.multiple_of(512 * k + 256, 256), 256), :] = jnp.zeros((256, 128), F32)
        return carry

    lax.fori_loop(0, cut.shape[0], clear, jnp.int32(0))
    stage[:, :, 512 * cut.shape[0] :, :] = jnp.zeros((2, 4, 256, 128), F32)
    pl.semaphore_wait(barrier, count)
    copies = outward(ext.at[0], send.at[0], recv.at[0])
    start_sides(copies["x"] + copies["y"] + copies["i"])
    take_sides(copies["x"])
    start_sides(copies["xy"])
    for c in loads:
        c.wait()
    arrange(amps, sort, arranged)
    take_sides(copies["y"])
    start_sides(copies["iy"])
    take_sides(copies["xy"] + copies["i"] + copies["iy"])
    leave_sides(sum(copies.values(), []))
    for step in range(2):
        old, now = ext.at[step], probes.at[step]
        cut_patches(positions, old, cut, total)
        weights[step].step(0)
        gradients(positions, cut, now, arranged, right, left, total, lhs_hi, lhs_lo, chi, stage, weights[step])
        update(step, positions, stage, grad, inbox.at[step], corners.at[step], acc, old, ext.at[1], now, probes.at[1], sums[step], weights[step], send, recv, obj_out, probe_out)


def update(step, positions, stage, grad, inbox, corners, acc, old, new, now, later, adder, heavy, send, recv, obj_out, probe_out):
    peak = jnp.max(now[0] * now[0] + now[1] * now[1])
    into = inward(grad, inbox, corners, send.at[1 + 2 * step], recv.at[1 + 2 * step])
    out = outward(new, send.at[2], recv.at[2]) if step == 0 else None
    core, up, down, outer = around()
    gx = lax.axis_index("gx")
    inner, halo = pl.ds(2 - core, 1), pl.ds(3 * core, 1)

    def add(where, target, place, value):
        @pl.when(where)
        def _():
            target[place] += value()

    def write(p, b, rows, x):
        if step == 1:
            probe_out[p, rows, 128 * b : 128 * b + 128] = x
        else:
            later[p, b, rows, :] = x

    for event in ORDERS[step]:
        if event in ("g0", "g1"):
            i = int(event[1])
            gather(positions, stage, grad, range(4), (TOP, BOTTOM)[i])
            start_sides([into["xy"][i], into["iy"][i], into["y"][i]])
        elif event == "g2":
            gather(positions, stage, grad, (0, 3), MIDDLE)
            start_sides(into["i"])
        elif event == "go":
            gather(positions, stage, grad, (1, 2), MIDDLE)
            acc[...] = grad[:, 1:3, MIDDLE, :]
        elif event == "b1":
            take_sides(into["iy"])
            add(up, grad, (slice(None), inner, TOP), lambda: corners[:, 2:3])
            add(down, grad, (slice(None), inner, BOTTOM), lambda: corners[:, 3:4])
            start_sides(into["z"])
        elif event == "b2":
            take_sides(into["xy"])
            add(down & outer, grad, (slice(None), halo, LOWER), lambda: corners[:, 0:1])
            add(up & outer, grad, (slice(None), halo, UPPER), lambda: corners[:, 1:2])
            start_sides(into["x"])
        elif event == "w":
            take_sides(into["y"] + into["z"] + into["i"] + into["x"])
            leave_sides(sum(into.values(), []))
            every = slice(None)
            add(down, acc, (every, every, slice(128, 256)), lambda: inbox[:, 1:3, TOP])
            add(up, acc, (every, every, slice(0, 128)), lambda: inbox[:, 1:3, BOTTOM])
            add(gx > 0, acc, (every, 0), lambda: inbox[:, 3, MIDDLE])
            add(gx < lax.axis_size("gx") - 1, acc, (every, 1), lambda: inbox[:, 0, MIDDLE])
        elif event == "c0":
            start_sides(out["x"] + out["y"] + out["i"])
        elif event == "c1":
            take_sides(out["x"])
            start_sides(out["xy"])
        elif event == "c2":
            take_sides(out["y"])
            start_sides(out["iy"])
        elif event == "cw":
            take_sides(out["xy"] + out["i"] + out["iy"])
            leave_sides(sum(out.values(), []))
        elif event[0] == "s":
            adder.step(int(event[1]))
        elif event[0] == "t":
            heavy.step(int(event[1]))
        elif event == "u" and step == 1:
            for b in range(2):
                obj_out[:, :, 128 * b : 128 * b + 128] = old[:, 1 + b, 128:384, :] + acc[:, b] / peak
        elif event == "u":
            new[:, 1:3, 128:384, :] = old[:, 1:3, 128:384, :] + acc[...] / peak
        else:
            new_probe(now, adder.full, heavy.full, write)


def shards(obj, probe, positions, amps):
    count = positions.shape[2]
    right, left = (jnp.asarray(t) for t in tables())
    tile = jax.ShapeDtypeStruct((2, 256, 256), F32)
    ext = (2, 4, 512, 128)
    anywhere = pl.BlockSpec(memory_space=pl.ANY)
    return pl.pallas_call(
        kernel,
        out_shape=(tile, tile),
        in_specs=[SMEM] + [VMEM] * 2 + [anywhere] * 4,
        out_specs=(VMEM, VMEM),
        scratch_shapes=[
            pltpu.VMEM((count, 256, 256), BF16),
            pltpu.VMEM((2, 2, 256, 256), BF16),
            pltpu.VMEM((2, 2, 256, 256), BF16),
            pltpu.VMEM((2, 256, 256), BF16),
            pltpu.SemaphoreType.DMA((4,)),
            pltpu.VMEM((2, *ext), F32),
            pltpu.VMEM(ext, F32),
            pltpu.VMEM((6, 256, 128), F32),
            pltpu.VMEM((2, 2, 256, 128), F32),
            pltpu.VMEM((2, 2, 2, 256, 128), F32),
            pltpu.VMEM((count, 256, 256), BF16),
            pltpu.VMEM((count, 2, 2, 256, 128), F32),
            pltpu.VMEM((2, 512, 256), BF16),
            pltpu.VMEM((2, 512, 256), BF16),
            pltpu.VMEM((2, 512, 256), F32),
            pltpu.VMEM((2, 4, 512 * count + 256, 128), F32),
            pltpu.VMEM((2, *ext), F32),
            pltpu.VMEM((2, 2, 4, 128, 128), F32),
            pltpu.SemaphoreType.DMA((4, 16)),
            pltpu.SemaphoreType.DMA((4, 16)),
            *sum_scratch(4) * 2,
            *sum_scratch(2) * 2,
        ],
        compiler_params=pltpu.CompilerParams(collective_id=0, has_side_effects=True, vmem_limit_bytes=VMEM_LIMIT),
        name="iterations",
    )(positions, obj, probe, amps, right, left, jnp.asarray(sorting()))


def solution(mesh):
    in_specs = (
        P(None, "gy", "gx"),
        P(),
        P("gy", "gx", None, None),
        P("gy", "gx", None, None, None),
    )
    out_specs = (P(None, "gy", "gx"), P())
    return jax.shard_map(shards, mesh=mesh, in_specs=in_specs, out_specs=out_specs, check_vma=False)
```

```python
import functools

import jax
import jax.numpy as jnp
import ml_dtypes
import numpy as np
from jax import lax
from jax.experimental import pallas as pl
from jax.experimental.pallas import tpu as pltpu
from jax.sharding import PartitionSpec as P

MESH = pl.DeviceIdType.MESH
F32 = jnp.float32
BF16 = jnp.bfloat16
VMEM = pl.BlockSpec(memory_space=pltpu.VMEM)
SMEM = pl.BlockSpec(memory_space=pltpu.SMEM)
VMEM_LIMIT = 60 * 1024 * 1024

TOP, UPPER, LOWER, BOTTOM = (slice(128 * i, 128 * i + 128) for i in range(4))
MIDDLE = slice(128, 384)


def tables():
    n = np.arange(128)[:, None]
    out = []
    for parity in range(2):
        turns = (n * (2 * np.arange(128)[None, :] + parity)) % 256
        angle = -2.0 * np.pi * turns / 256.0
        re, im = np.cos(angle) / 16.0, np.sin(angle) / 16.0
        m = np.block([[re, im], [-im, re]]).astype(np.float32)
        hi = m.astype(ml_dtypes.bfloat16)
        lo = (m - hi.astype(np.float32)).astype(ml_dtypes.bfloat16)
        out.append(np.stack([hi, lo]))
    right = np.stack(out)
    return right, np.ascontiguousarray(np.swapaxes(right, 2, 3))


def sorting():
    m = np.zeros((256, 256), np.float32)
    m[np.arange(256), np.concatenate([np.arange(0, 256, 2), np.arange(1, 256, 2)])] = 1.0
    return np.stack([m, m.T]).astype(ml_dtypes.bfloat16)


def around():
    gy, gx = lax.axis_index("gy"), lax.axis_index("gx")
    core = lax.rem(gx, 2)
    outer = jnp.where(core == 0, gx > 0, gx < lax.axis_size("gx") - 1)
    return core, gy > 0, gy < lax.axis_size("gy") - 1, outer


def devices_around():
    gy, gx = lax.axis_index("gy"), lax.axis_index("gx")
    core = lax.rem(gx, 2)
    ny, nx = lax.axis_size("gy"), lax.axis_size("gx")
    return (
        (jnp.maximum(gy - 1, 0), gx),
        (jnp.minimum(gy + 1, ny - 1), gx),
        (gy, jnp.clip(gx + 2 * core - 1, 0, nx - 1)),
        (gy, gx + 1 - 2 * core),
    )


def greet_sides():
    barrier = pltpu.get_barrier_semaphore()
    count = jnp.int32(0)
    for ok, device in zip(around()[1:], devices_around()):

        @pl.when(ok)
        def _(device=device):
            pl.semaphore_signal(barrier, inc=1, device_id=device, device_id_type=MESH)

        count = count + ok.astype(jnp.int32)
    return barrier, count


def sides(send, recv):
    slots = iter(range(16))

    def link(goes, comes, source, target, device):
        i = next(slots)
        return (
            goes,
            comes,
            pltpu.make_async_remote_copy(
                source, target, send.at[i], recv.at[i], device_id=device, device_id_type=MESH
            ),
        )

    return link


def outward(ext, send, recv):
    core, up, down, outer = around()
    above, below, beside, other = devices_around()
    link = sides(send, recv)
    edge, inner = pl.ds(1 + core, 1), pl.ds(2 - core, 1)
    halo, far = pl.ds(3 * core, 1), pl.ds(3 - 3 * core, 1)
    always = up | jnp.logical_not(up)
    return {
        "y": [
            link(up, down, ext.at[:, 1:3, UPPER], ext.at[:, 1:3, BOTTOM], above),
            link(down, up, ext.at[:, 1:3, LOWER], ext.at[:, 1:3, TOP], below),
        ],
        "x": [link(outer, outer, ext.at[:, edge, MIDDLE], ext.at[:, far, MIDDLE], beside)],
        "i": [link(always, always, ext.at[:, inner, MIDDLE], ext.at[:, halo, MIDDLE], other)],
        "xy": [
            link(up & outer, down & outer, ext.at[:, halo, UPPER], ext.at[:, halo, BOTTOM], above),
            link(down & outer, up & outer, ext.at[:, halo, LOWER], ext.at[:, halo, TOP], below),
        ],
        "iy": [
            link(up, up, ext.at[:, inner, TOP], ext.at[:, halo, TOP], other),
            link(down, down, ext.at[:, inner, BOTTOM], ext.at[:, halo, BOTTOM], other),
        ],
    }


def inward(grad, box, corners, send, recv):
    core, up, down, outer = around()
    above, below, beside, other = devices_around()
    link = sides(send, recv)
    edge, inner = pl.ds(1 + core, 1), pl.ds(2 - core, 1)
    halo, far = pl.ds(3 * core, 1), pl.ds(3 - 3 * core, 1)
    always = up | jnp.logical_not(up)
    return {
        "xy": [
            link(up & outer, down & outer, grad.at[:, halo, TOP], corners.at[:, 0:1], above),
            link(down & outer, up & outer, grad.at[:, halo, BOTTOM], corners.at[:, 1:2], below),
        ],
        "iy": [
            link(up, up, grad.at[:, far, TOP], corners.at[:, 2:3], other),
            link(down, down, grad.at[:, far, BOTTOM], corners.at[:, 3:4], other),
        ],
        "y": [
            link(up, down, grad.at[:, edge, TOP], box.at[:, edge, TOP], above),
            link(down, up, grad.at[:, edge, BOTTOM], box.at[:, edge, BOTTOM], below),
        ],
        "z": [
            link(up, down, grad.at[:, inner, TOP], box.at[:, inner, TOP], above),
            link(down, up, grad.at[:, inner, BOTTOM], box.at[:, inner, BOTTOM], below),
        ],
        "i": [link(always, always, grad.at[:, far, MIDDLE], box.at[:, far, MIDDLE], other)],
        "x": [link(outer, outer, grad.at[:, halo, MIDDLE], box.at[:, halo, MIDDLE], beside)],
    }


def start_sides(copies):
    for ok, _, copy in copies:
        pl.when(ok)(copy.start)


def take_sides(copies):
    for _, arrives, copy in copies:
        pl.when(arrives)(copy.wait_recv)


def leave_sides(copies):
    for ok, _, copy in copies:
        pl.when(ok)(copy.wait_send)


def blank_outside(ext):
    gy, gx = lax.axis_index("gy"), lax.axis_index("gx")
    for outside, place in (
        (gy == 0, (slice(0, 4), TOP)),
        (gy == lax.axis_size("gy") - 1, (slice(0, 4), BOTTOM)),
        (gx == 0, (slice(0, 1), slice(0, 512))),
        (gx == lax.axis_size("gx") - 1, (slice(3, 4), slice(0, 512))),
    ):

        @pl.when(outside)
        def _(place=place):
            cols, rows = place
            ext[:, cols, rows, :] = jnp.zeros((2, cols.stop - cols.start, rows.stop - rows.start, 128), F32)


def arrange(amps, sort, out):
    def one(k, carry):
        half = jnp.dot(sort[0], amps[k], preferred_element_type=F32).astype(BF16)
        out[k] = jnp.dot(half, sort[1], preferred_element_type=F32).astype(BF16)
        return carry

    lax.fori_loop(0, out.shape[0], one, jnp.int32(0))


def split(x):
    hi = x.astype(BF16)
    return hi, (x - hi.astype(F32)).astype(BF16)


def right_dot(hi, lo, m):
    return jnp.dot(
        jnp.concatenate([hi, lo, hi], axis=1),
        jnp.concatenate([m[0], m[0], m[1]], axis=0),
        preferred_element_type=F32,
    )


def left_dot(m, hi, lo):
    first = jnp.dot(jnp.concatenate([m[0], m[1]], axis=0), hi, preferred_element_type=F32)
    return first[:256] + (first[256:] + jnp.dot(m[0], lo, preferred_element_type=F32))


def corner(positions, k):
    row = positions[0, 0, 0, k] - lax.axis_index("gy") * 256 + 128
    col = positions[0, 0, 1, k] - lax.axis_index("gx") * 256 + 128
    return jnp.clip(row, 0, 255), jnp.clip(col, 0, 255)


def cut_patches(positions, ext, cut, total):
    total[4:6] = jnp.zeros((2, 256, 128), F32)
    lane = lax.broadcasted_iota(jnp.int32, (1, 128), 1)

    def visit(k, carry):
        r, c = corner(positions, k)
        first = lax.div(c, 128)
        c = lax.rem(c, 128)
        back = lax.rem(128 - c, 128)
        keep = lane < 128 - c
        for i in range(0, 256, 64):
            rows = slice(i, i + 64)
            part = []
            for p in range(2):
                t = [pltpu.roll(ext[p, first + b, pl.ds(r + i, 64), :], back, 1) for b in range(3)]
                h = [jnp.where(keep, t[0], t[1]), jnp.where(keep, t[1], t[2])]
                for b in range(2):
                    cut[k, p, b, rows, :] = h[b]
                part.append(h)
            for b in range(2):
                total[4 + b, rows, :] += part[0][b] * part[0][b] + part[1][b] * part[1][b]
        return carry

    lax.fori_loop(0, cut.shape[0], visit, jnp.int32(0))


def gradients(positions, cut, probe, amps, right, left, total, lhs_hi, lhs_lo, chi, stage, heavy):
    total[0:4] = jnp.zeros((4, 256, 128), F32)
    chi[...] = jnp.zeros_like(chi)
    lane = lax.broadcasted_iota(jnp.int32, (1, 128), 1)
    pairs = cut.shape[0] // 2

    def waves(k, u):
        for i in range(0, 256, 64):
            rows = slice(i, i + 64)
            place = slice(256 * u + i, 256 * u + i + 64)
            wave = []
            for b in range(2):
                ore, oim = cut[k, 0, b, rows, :], cut[k, 1, b, rows, :]
                pre, pim = probe[0, b, rows, :], probe[1, b, rows, :]
                wave.append((pre * ore - pim * oim, pre * oim + pim * ore))
            for q in range(2):
                for p in range(2):
                    x = wave[0][p] + wave[1][p] if q == 0 else wave[0][p] - wave[1][p]
                    hi, lo = split(x)
                    lhs_hi[q, place, 128 * p : 128 * p + 128] = hi
                    lhs_lo[q, place, 128 * p : 128 * p + 128] = lo

    def correct(k, s, top, low):
        hi, lo = split(top + low if s == 0 else top - low)
        far = left_dot(left[s], hi, lo)
        re, im = far[:128], far[128:]
        factor = amps[k, 128 * s : 128 * s + 128, :].astype(F32) * lax.rsqrt(jnp.maximum(re * re + im * im, 0.25)) - 1.0
        hi, lo = split(jnp.concatenate([re * factor, im * factor], axis=0))
        return left_dot(right[s], hi, lo)

    def deposit(k, u):
        c = lax.rem(corner(positions, k)[1], 128)
        late = lane >= c
        for i in range(0, 256, 64):
            rows = slice(i, i + 64)
            place = slice(256 * u + i, 256 * u + i + 64)
            even, odd = chi[0, place, :], chi[1, place, :]
            g = [[], []]
            for b in range(2):
                x = even + odd if b == 0 else even - odd
                cre, cim = x[:, :128], x[:, 128:]
                pre, pim = probe[0, b, rows, :], probe[1, b, rows, :]
                ore, oim = cut[k, 0, b, rows, :], cut[k, 1, b, rows, :]
                total[b, rows, :] += ore * cre + oim * cim
                total[2 + b, rows, :] += ore * cim - oim * cre
                g[0].append(pltpu.roll(pre * cre + pim * cim, c, 1))
                g[1].append(pltpu.roll(pre * cim - pim * cre, c, 1))
            for p in range(2):
                to = pl.ds(pl.multiple_of(512 * k + 256 + i, 64), 64)
                stage[p, 1, to, :] = jnp.where(late, g[p][0], 0.0)
                stage[p, 2, to, :] = jnp.where(late, g[p][1], g[p][0])
                stage[p, 3, to, :] = jnp.where(late, 0.0, g[p][1])

    def stack(y, u):
        out = []
        for h in range(2):
            rows = slice(256 * u + 128 * h, 256 * u + 128 * h + 128)
            parts = [
                jnp.concatenate([y[0][rows, lanes], y[1][rows, lanes]], axis=1)
                for lanes in (slice(0, 128), slice(128, 256))
            ]
            out.append(jnp.concatenate(parts, axis=0))
        return out

    def visit(j, carry):
        pl.when(j == 1)(functools.partial(heavy.step, 1))
        pl.when(j == pairs - 1)(functools.partial(heavy.step, 2))
        y = [right_dot(lhs_hi[q], lhs_lo[q], right[q]) for q in range(2)]
        for u in range(2):
            deposit(2 * jnp.maximum(j - 1, 0) + u, u)
        half = [[], []]
        for s in range(2):
            for u in range(2):
                top, low = stack(y, u)
                half[u].append(correct(2 * j + u, s, top, low))
        for q in range(2):
            lanes = slice(128 * q, 128 * q + 128)
            parts = []
            for u in range(2):
                for x in (half[u][0] + half[u][1], half[u][0] - half[u][1]):
                    parts.append(jnp.concatenate([x[:128, lanes], x[128:, lanes]], axis=1))
            hi, lo = split(jnp.concatenate(parts, axis=0))
            chi[q] = right_dot(hi, lo, left[q])
        for u in range(2):
            waves(2 * jnp.minimum(j + 1, pairs - 1) + u, u)
        return carry

    for u in range(2):
        waves(u, u)
    lax.fori_loop(0, pairs, visit, jnp.int32(0))
    for u in range(2):
        deposit(2 * pairs - 2 + u, u)


def gather(positions, stage, grad, cols, rows):
    def part(i, carry):
        start = pl.multiple_of(i * 64, 64)
        for p in range(2):
            for b in cols:
                x = jnp.zeros((64, 128), F32)
                for k in range(stage.shape[2] // 512):
                    r, c = corner(positions, k)
                    x = x + stage[p, lax.rem(b + 1 - lax.div(c, 128), 4), pl.ds(512 * k + 256 + start - r, 64), :]
                grad[p, b, pl.ds(start, 64), :] = x
        return carry

    lax.fori_loop(rows.start // 64, rows.stop // 64, part, jnp.int32(0))


def sibling():
    gy, gx = lax.axis_index("gy"), lax.axis_index("gx")
    return gy, gx + 1 - 2 * lax.rem(gx, 2)


def along_x(d):
    gy, gx = lax.axis_index("gy"), lax.axis_index("gx")
    x = lax.div(gx, 4)
    return gy, lax.rem(x + d, 4) * 4 + lax.rem(gx, 4)


def member(j):
    gx = lax.axis_index("gx")
    place = lax.rem(j, 8)
    return lax.div(j, 8) * 4 + lax.div(place, 2), lax.div(gx, 4) * 4 + lax.rem(place, 2) * 2 + lax.rem(gx, 2)


class Sum:
    def __init__(self, total, full, acc0, acc1, acc2, rb0, rb1, rb2, send, recv):
        self.total, self.full, self.acc0, self.acc1, self.acc2 = total, full, acc0, acc1, acc2
        self.rb0, self.rb1, self.rb2 = rb0, rb1, rb2
        self.send, self.recv = send, recv
        gy, gx = lax.axis_index("gy"), lax.axis_index("gx")
        self.core, self.x = lax.rem(gx, 2), lax.div(gx, 4)
        self.mine = lax.rem(gy, 4) * 2 + lax.div(lax.rem(gx, 4), 2)
        self.me = lax.div(gy, 4) * 8 + self.mine
        self.tiles = total.shape[0] // 2

    def greet(self, barrier):
        devices = [sibling()] + [along_x(d) for d in (1, 2, 3)] + [member(lax.rem(self.me + d, 16)) for d in range(1, 16)]
        for device in devices:
            pl.semaphore_signal(barrier, inc=1, device_id=device, device_id_type=MESH)
        return len(devices)

    def copy(self, source, target, i, device):
        return pltpu.make_async_remote_copy(
            source, target, self.send.at[i], self.recv.at[i], device_id=device, device_id_type=MESH
        )

    def copies0(self):
        theirs = pl.ds(pl.multiple_of((1 - self.core) * 128, 128), 128)
        return [self.copy(self.total.at[:, theirs, :], self.rb0, 0, sibling())]

    def copies1(self):
        out = []
        for d in (1, 2, 3):
            part = pl.ds(pl.multiple_of(lax.rem(self.x + d, 4) * 32, 32), 32)
            out.append(self.copy(self.acc0.at[:, part, :], self.rb1.at[d - 1], d, along_x(d)))
        return out

    def copies2(self):
        out = []
        for d in range(1, 16):
            to = lax.rem(self.me + d, 16)
            part = pl.ds(lax.rem(to, 8) * self.tiles, self.tiles)
            out.append(self.copy(self.acc1.at[part], self.rb2.at[self.me], 3 + d, member(to)))
        return out

    def copies3(self):
        place = self.full.at[self.core, self.x, pl.ds(self.mine * self.tiles, self.tiles)]
        out = []
        for d in range(1, 8):
            to = lax.rem(self.mine + d, 8) + lax.div(self.me, 8) * 8
            out.append(self.copy(self.acc2, place, 18 + d, member(to)))
        return out

    def copies4(self):
        place = self.full.at[self.core, self.x]
        return [self.copy(place, place, 25 + d, along_x(d)) for d in (1, 2, 3)]

    def copies5(self):
        place = self.full.at[self.core]
        return [self.copy(place, place, 29, sibling())]

    def step(self, number):
        if number > 0:
            for c in getattr(self, f"copies{number - 1}")():
                c.wait_recv()
        if number == 1:
            own = pl.ds(pl.multiple_of(self.core * 128, 128), 128)
            self.acc0[...] = self.total[:, own, :] + self.rb0[...]
        if number == 2:
            own = pl.ds(pl.multiple_of(self.x * 32, 32), 32)
            x = self.acc0[:, own, :] + self.rb1[0] + self.rb1[1] + self.rb1[2]
            self.acc1[...] = x.reshape(self.acc1.shape)
            self.rb2[pl.ds(self.me, 1)] = self.acc1[pl.ds(self.mine * self.tiles, self.tiles)][None]
        if number == 3:
            x = self.rb2[0]
            for j in range(1, 16):
                x = x + self.rb2[j]
            self.acc2[...] = x
            self.full[pl.ds(self.core, 1), pl.ds(self.x, 1), pl.ds(self.mine * self.tiles, self.tiles)] = x[None, None]
        if number < 6:
            for c in getattr(self, f"copies{number}")():
                c.start()
        else:
            for stage in range(6):
                for c in getattr(self, f"copies{stage}")():
                    c.wait_send()


def sum_scratch(n):
    return [
        pltpu.VMEM((2, 4, 4 * n, 8, 128), F32),
        pltpu.VMEM((n, 128, 128), F32),
        pltpu.VMEM((4 * n, 8, 128), F32),
        pltpu.VMEM((n // 2, 8, 128), F32),
        pltpu.VMEM((n, 128, 128), F32),
        pltpu.VMEM((3, n, 32, 128), F32),
        pltpu.VMEM((16, n // 2, 8, 128), F32),
        pltpu.SemaphoreType.DMA((30,)),
        pltpu.SemaphoreType.DMA((30,)),
    ]


def new_probe(probe, full, weight, write):
    parts = [weight[h, x] for h in range(2) for x in range(4)]
    top = parts[0]
    for w in parts[1:]:
        top = jnp.maximum(top, w)
    floor = 0.1 * jnp.max(top)
    for h in range(2):
        for x in range(4):
            rows = slice(128 * h + 32 * x, 128 * h + 32 * x + 32)
            for b in range(2):
                w = 0.9 * weight[h, x, 4 * b : 4 * b + 4].reshape(32, 128) + floor
                for p in range(2):
                    g = full[h, x, 8 * p + 4 * b : 8 * p + 4 * b + 4].reshape(32, 128)
                    write(p, b, rows, probe[p, b, rows, :] + g / w)


ORDERS = (
    ("s0", "g0", "s1", "g1", "g2", "t3", "go", "s2", "b1", "b2", "t4", "s3", "t5", "s4", "w", "u", "c0", "s5", "c1", "c2", "s6", "t6", "p", "cw"),
    ("s0", "g0", "s1", "g1", "g2", "t3", "go", "s2", "b1", "b2", "t4", "s3", "t5", "s4", "w", "u", "s5", "s6", "t6", "p"),
)


def kernel(positions, obj, probe, amps_far, right_far, left_far, sort_far, obj_out, probe_out, *refs):
    amps, right, left, sort, load, ext, grad, total, acc, probes, arranged, cut, lhs_hi, lhs_lo, chi, stage, inbox, corners, send, recv, *rest = refs
    size = len(rest) // 4
    parts = [rest[size * i : size * (i + 1)] for i in range(4)]
    sums = [Sum(total.at[0:4], *parts[step]) for step in range(2)]
    weights = [Sum(total.at[4:6], *parts[2 + step]) for step in range(2)]
    loads = [
        pltpu.make_async_copy(source, target, load.at[i])
        for i, (source, target) in enumerate(
            ((amps_far.at[0, 0], amps), (sort_far, sort), (right_far, right), (left_far, left))
        )
    ]
    for c in loads:
        c.start()
    for step in range(2):
        blank_outside(ext.at[step])
    barrier, count = greet_sides()
    count = count + sums[0].greet(barrier)
    for b in range(2):
        lanes = slice(128 * b, 128 * b + 128)
        ext[0, :, 1 + b, 128:384, :] = obj[:, :, lanes]
        probes[0, :, b] = probe[:, :, lanes]

    def clear(k, carry):
        for p in range(2):
            for b in range(4):
                stage[p, b, pl.ds(pl.multiple_of(512 * k, 512), 256), :] = jnp.zeros((256, 128), F32)
            stage[p, 0, pl.ds(pl.multiple_of(512 * k + 256, 256), 256), :] = jnp.zeros((256, 128), F32)
        return carry

    lax.fori_loop(0, cut.shape[0], clear, jnp.int32(0))
    stage[:, :, 512 * cut.shape[0] :, :] = jnp.zeros((2, 4, 256, 128), F32)
    pl.semaphore_wait(barrier, count)
    copies = outward(ext.at[0], send.at[0], recv.at[0])
    start_sides(copies["x"] + copies["y"] + copies["i"])
    take_sides(copies["x"])
    start_sides(copies["xy"])
    for c in loads:
        c.wait()
    arrange(amps, sort, arranged)
    take_sides(copies["y"])
    start_sides(copies["iy"])
    take_sides(copies["xy"] + copies["i"] + copies["iy"])
    leave_sides(sum(copies.values(), []))
    for step in range(2):
        old, now = ext.at[step], probes.at[step]
        cut_patches(positions, old, cut, total)
        weights[step].step(0)
        gradients(positions, cut, now, arranged, right, left, total, lhs_hi, lhs_lo, chi, stage, weights[step])
        update(step, positions, stage, grad, inbox.at[step], corners.at[step], acc, old, ext.at[1], now, probes.at[1], sums[step], weights[step], send, recv, obj_out, probe_out)


def update(step, positions, stage, grad, inbox, corners, acc, old, new, now, later, adder, heavy, send, recv, obj_out, probe_out):
    peak = jnp.max(now[0] * now[0] + now[1] * now[1])
    into = inward(grad, inbox, corners, send.at[1 + 2 * step], recv.at[1 + 2 * step])
    out = outward(new, send.at[2], recv.at[2]) if step == 0 else None
    core, up, down, outer = around()
    gx = lax.axis_index("gx")
    inner, halo = pl.ds(2 - core, 1), pl.ds(3 * core, 1)

    def add(where, target, place, value):
        @pl.when(where)
        def _():
            target[place] += value()

    def write(p, b, rows, x):
        if step == 1:
            probe_out[p, rows, 128 * b : 128 * b + 128] = x
        else:
            later[p, b, rows, :] = x

    for event in ORDERS[step]:
        if event in ("g0", "g1"):
            i = int(event[1])
            gather(positions, stage, grad, range(4), (TOP, BOTTOM)[i])
            start_sides([into["xy"][i], into["iy"][i], into["y"][i]])
        elif event == "g2":
            gather(positions, stage, grad, (0, 3), MIDDLE)
            start_sides(into["i"])
        elif event == "go":
            gather(positions, stage, grad, (1, 2), MIDDLE)
            acc[...] = grad[:, 1:3, MIDDLE, :]
        elif event == "b1":
            take_sides(into["iy"])
            add(up, grad, (slice(None), inner, TOP), lambda: corners[:, 2:3])
            add(down, grad, (slice(None), inner, BOTTOM), lambda: corners[:, 3:4])
            start_sides(into["z"])
        elif event == "b2":
            take_sides(into["xy"])
            add(down & outer, grad, (slice(None), halo, LOWER), lambda: corners[:, 0:1])
            add(up & outer, grad, (slice(None), halo, UPPER), lambda: corners[:, 1:2])
            start_sides(into["x"])
        elif event == "w":
            take_sides(into["y"] + into["z"] + into["i"] + into["x"])
            leave_sides(sum(into.values(), []))
            every = slice(None)
            add(down, acc, (every, every, slice(128, 256)), lambda: inbox[:, 1:3, TOP])
            add(up, acc, (every, every, slice(0, 128)), lambda: inbox[:, 1:3, BOTTOM])
            add(gx > 0, acc, (every, 0), lambda: inbox[:, 3, MIDDLE])
            add(gx < lax.axis_size("gx") - 1, acc, (every, 1), lambda: inbox[:, 0, MIDDLE])
        elif event == "c0":
            start_sides(out["x"] + out["y"] + out["i"])
        elif event == "c1":
            take_sides(out["x"])
            start_sides(out["xy"])
        elif event == "c2":
            take_sides(out["y"])
            start_sides(out["iy"])
        elif event == "cw":
            take_sides(out["xy"] + out["i"] + out["iy"])
            leave_sides(sum(out.values(), []))
        elif event[0] == "s":
            adder.step(int(event[1]))
        elif event[0] == "t":
            heavy.step(int(event[1]))
        elif event == "u" and step == 1:
            for b in range(2):
                obj_out[:, :, 128 * b : 128 * b + 128] = old[:, 1 + b, 128:384, :] + acc[:, b] / peak
        elif event == "u":
            new[:, 1:3, 128:384, :] = old[:, 1:3, 128:384, :] + acc[...] / peak
        else:
            new_probe(now, adder.full, heavy.full, write)


def shards(obj, probe, positions, amps):
    count = positions.shape[2]
    right, left = (jnp.asarray(t) for t in tables())
    tile = jax.ShapeDtypeStruct((2, 256, 256), F32)
    ext = (2, 4, 512, 128)
    anywhere = pl.BlockSpec(memory_space=pl.ANY)
    return pl.pallas_call(
        kernel,
        out_shape=(tile, tile),
        in_specs=[SMEM] + [VMEM] * 2 + [anywhere] * 4,
        out_specs=(VMEM, VMEM),
        scratch_shapes=[
            pltpu.VMEM((count, 256, 256), BF16),
            pltpu.VMEM((2, 2, 256, 256), BF16),
            pltpu.VMEM((2, 2, 256, 256), BF16),
            pltpu.VMEM((2, 256, 256), BF16),
            pltpu.SemaphoreType.DMA((4,)),
            pltpu.VMEM((2, *ext), F32),
            pltpu.VMEM(ext, F32),
            pltpu.VMEM((6, 256, 128), F32),
            pltpu.VMEM((2, 2, 256, 128), F32),
            pltpu.VMEM((2, 2, 2, 256, 128), F32),
            pltpu.VMEM((count, 256, 256), BF16),
            pltpu.VMEM((count, 2, 2, 256, 128), F32),
            pltpu.VMEM((2, 512, 256), BF16),
            pltpu.VMEM((2, 512, 256), BF16),
            pltpu.VMEM((2, 512, 256), F32),
            pltpu.VMEM((2, 4, 512 * count + 256, 128), F32),
            pltpu.VMEM((2, *ext), F32),
            pltpu.VMEM((2, 2, 4, 128, 128), F32),
            pltpu.SemaphoreType.DMA((4, 16)),
            pltpu.SemaphoreType.DMA((4, 16)),
            *sum_scratch(4) * 2,
            *sum_scratch(2) * 2,
        ],
        compiler_params=pltpu.CompilerParams(collective_id=0, has_side_effects=True, vmem_limit_bytes=VMEM_LIMIT),
        name="iterations",
    )(jnp.swapaxes(positions, 2, 3), obj, probe, amps, right, left, jnp.asarray(sorting()))


def solution(mesh):
    in_specs = (
        P(None, "gy", "gx"),
        P(),
        P("gy", "gx", None, None),
        P("gy", "gx", None, None, None),
    )
    out_specs = (P(None, "gy", "gx"), P())
    return jax.shard_map(shards, mesh=mesh, in_specs=in_specs, out_specs=out_specs, check_vma=False)
```

```python
import functools

import jax
import jax.numpy as jnp
import ml_dtypes
import numpy as np
from jax import lax
from jax.experimental import pallas as pl
from jax.experimental.pallas import tpu as pltpu
from jax.sharding import PartitionSpec as P

MESH = pl.DeviceIdType.MESH
F32 = jnp.float32
BF16 = jnp.bfloat16
VMEM = pl.BlockSpec(memory_space=pltpu.VMEM)
SMEM = pl.BlockSpec(memory_space=pltpu.SMEM)
VMEM_LIMIT = 60 * 1024 * 1024

TOP, UPPER, LOWER, BOTTOM = (slice(128 * i, 128 * i + 128) for i in range(4))
MIDDLE = slice(128, 384)


def tables():
    n = np.arange(128)[:, None]
    out = []
    for parity in range(2):
        turns = (n * (2 * np.arange(128)[None, :] + parity)) % 256
        angle = -2.0 * np.pi * turns / 256.0
        re, im = np.cos(angle) / 16.0, np.sin(angle) / 16.0
        m = np.block([[re, im], [-im, re]]).astype(np.float32)
        hi = m.astype(ml_dtypes.bfloat16)
        lo = (m - hi.astype(np.float32)).astype(ml_dtypes.bfloat16)
        out.append(np.stack([hi, lo]))
    right = np.stack(out)
    return right, np.ascontiguousarray(np.swapaxes(right, 2, 3))


def sorting():
    m = np.zeros((256, 256), np.float32)
    m[np.arange(256), np.concatenate([np.arange(0, 256, 2), np.arange(1, 256, 2)])] = 1.0
    return np.stack([m, m.T]).astype(ml_dtypes.bfloat16)


def around():
    gy, gx = lax.axis_index("gy"), lax.axis_index("gx")
    core = lax.rem(gx, 2)
    outer = jnp.where(core == 0, gx > 0, gx < lax.axis_size("gx") - 1)
    return core, gy > 0, gy < lax.axis_size("gy") - 1, outer


def devices_around():
    gy, gx = lax.axis_index("gy"), lax.axis_index("gx")
    core = lax.rem(gx, 2)
    ny, nx = lax.axis_size("gy"), lax.axis_size("gx")
    return (
        (jnp.maximum(gy - 1, 0), gx),
        (jnp.minimum(gy + 1, ny - 1), gx),
        (gy, jnp.clip(gx + 2 * core - 1, 0, nx - 1)),
        (gy, gx + 1 - 2 * core),
    )


def greet_sides():
    barrier = pltpu.get_barrier_semaphore()
    count = jnp.int32(0)
    for ok, device in zip(around()[1:], devices_around()):

        @pl.when(ok)
        def _(device=device):
            pl.semaphore_signal(barrier, inc=1, device_id=device, device_id_type=MESH)

        count = count + ok.astype(jnp.int32)
    return barrier, count


def sides(send, recv):
    slots = iter(range(16))

    def link(goes, comes, source, target, device):
        i = next(slots)
        return (
            goes,
            comes,
            pltpu.make_async_remote_copy(
                source, target, send.at[i], recv.at[i], device_id=device, device_id_type=MESH
            ),
        )

    return link


def outward(ext, send, recv):
    core, up, down, outer = around()
    above, below, beside, other = devices_around()
    link = sides(send, recv)
    edge, inner = pl.ds(1 + core, 1), pl.ds(2 - core, 1)
    halo, far = pl.ds(3 * core, 1), pl.ds(3 - 3 * core, 1)
    always = up | jnp.logical_not(up)
    return {
        "y": [
            link(up, down, ext.at[:, 1:3, UPPER], ext.at[:, 1:3, BOTTOM], above),
            link(down, up, ext.at[:, 1:3, LOWER], ext.at[:, 1:3, TOP], below),
        ],
        "x": [link(outer, outer, ext.at[:, edge, MIDDLE], ext.at[:, far, MIDDLE], beside)],
        "i": [link(always, always, ext.at[:, inner, MIDDLE], ext.at[:, halo, MIDDLE], other)],
        "xy": [
            link(up & outer, down & outer, ext.at[:, halo, UPPER], ext.at[:, halo, BOTTOM], above),
            link(down & outer, up & outer, ext.at[:, halo, LOWER], ext.at[:, halo, TOP], below),
        ],
        "iy": [
            link(up, up, ext.at[:, inner, TOP], ext.at[:, halo, TOP], other),
            link(down, down, ext.at[:, inner, BOTTOM], ext.at[:, halo, BOTTOM], other),
        ],
    }


def inward(grad, box, corners, send, recv):
    core, up, down, outer = around()
    above, below, beside, other = devices_around()
    link = sides(send, recv)
    edge, inner = pl.ds(1 + core, 1), pl.ds(2 - core, 1)
    halo, far = pl.ds(3 * core, 1), pl.ds(3 - 3 * core, 1)
    always = up | jnp.logical_not(up)
    return {
        "xy": [
            link(up & outer, down & outer, grad.at[:, halo, TOP], corners.at[:, 0:1], above),
            link(down & outer, up & outer, grad.at[:, halo, BOTTOM], corners.at[:, 1:2], below),
        ],
        "iy": [
            link(up, up, grad.at[:, far, TOP], corners.at[:, 2:3], other),
            link(down, down, grad.at[:, far, BOTTOM], corners.at[:, 3:4], other),
        ],
        "y": [
            link(up, down, grad.at[:, edge, TOP], box.at[:, edge, TOP], above),
            link(down, up, grad.at[:, edge, BOTTOM], box.at[:, edge, BOTTOM], below),
        ],
        "z": [
            link(up, down, grad.at[:, inner, TOP], box.at[:, inner, TOP], above),
            link(down, up, grad.at[:, inner, BOTTOM], box.at[:, inner, BOTTOM], below),
        ],
        "i": [link(always, always, grad.at[:, far, MIDDLE], box.at[:, far, MIDDLE], other)],
        "x": [link(outer, outer, grad.at[:, halo, MIDDLE], box.at[:, halo, MIDDLE], beside)],
    }


def start_sides(copies):
    for ok, _, copy in copies:
        pl.when(ok)(copy.start)


def take_sides(copies):
    for _, arrives, copy in copies:
        pl.when(arrives)(copy.wait_recv)


def leave_sides(copies):
    for ok, _, copy in copies:
        pl.when(ok)(copy.wait_send)


def blank_outside(ext):
    gy, gx = lax.axis_index("gy"), lax.axis_index("gx")
    for outside, place in (
        (gy == 0, (slice(0, 4), TOP)),
        (gy == lax.axis_size("gy") - 1, (slice(0, 4), BOTTOM)),
        (gx == 0, (slice(0, 1), slice(0, 512))),
        (gx == lax.axis_size("gx") - 1, (slice(3, 4), slice(0, 512))),
    ):

        @pl.when(outside)
        def _(place=place):
            cols, rows = place
            ext[:, cols, rows, :] = jnp.zeros((2, cols.stop - cols.start, rows.stop - rows.start, 128), F32)


def arrange(amps, sort, out):
    def one(k, carry):
        half = jnp.dot(sort[0], amps[k], preferred_element_type=F32).astype(BF16)
        out[k] = jnp.dot(half, sort[1], preferred_element_type=F32).astype(BF16)
        return carry

    lax.fori_loop(0, out.shape[0], one, jnp.int32(0))


def split(x):
    hi = x.astype(BF16)
    return hi, (x - hi.astype(F32)).astype(BF16)


def right_dot(hi, lo, m):
    rows = hi.shape[0]
    first = jnp.dot(jnp.concatenate([hi, lo], axis=0), m[0], preferred_element_type=F32)
    return first[:rows] + (first[rows:] + jnp.dot(hi, m[1], preferred_element_type=F32))


def left_dot(m, hi, lo):
    first = jnp.dot(jnp.concatenate([m[0], m[1]], axis=0), hi, preferred_element_type=F32)
    return first[:256] + (first[256:] + jnp.dot(m[0], lo, preferred_element_type=F32))


def corner(positions, k):
    row = positions[0, 0, 0, k] - lax.axis_index("gy") * 256 + 128
    col = positions[0, 0, 1, k] - lax.axis_index("gx") * 256 + 128
    return jnp.clip(row, 0, 255), jnp.clip(col, 0, 255)


def cut_patches(positions, ext, cut, total):
    total[4:6] = jnp.zeros((2, 256, 128), F32)
    lane = lax.broadcasted_iota(jnp.int32, (1, 128), 1)

    def visit(k, carry):
        r, c = corner(positions, k)
        first = lax.div(c, 128)
        c = lax.rem(c, 128)
        back = lax.rem(128 - c, 128)
        keep = lane < 128 - c
        for i in range(0, 256, 64):
            rows = slice(i, i + 64)
            part = []
            for p in range(2):
                t = [pltpu.roll(ext[p, first + b, pl.ds(r + i, 64), :], back, 1) for b in range(3)]
                h = [jnp.where(keep, t[0], t[1]), jnp.where(keep, t[1], t[2])]
                for b in range(2):
                    cut[k, p, b, rows, :] = h[b]
                part.append(h)
            for b in range(2):
                total[4 + b, rows, :] += part[0][b] * part[0][b] + part[1][b] * part[1][b]
        return carry

    lax.fori_loop(0, cut.shape[0], visit, jnp.int32(0))


def gradients(positions, cut, probe, amps, right, left, total, lhs_hi, lhs_lo, chi, stage, heavy):
    total[0:4] = jnp.zeros((4, 256, 128), F32)
    chi[...] = jnp.zeros_like(chi)
    lane = lax.broadcasted_iota(jnp.int32, (1, 128), 1)
    pairs = cut.shape[0] // 2

    def waves(k, u):
        for i in range(0, 256, 64):
            rows = slice(i, i + 64)
            place = slice(256 * u + i, 256 * u + i + 64)
            wave = []
            for b in range(2):
                ore, oim = cut[k, 0, b, rows, :], cut[k, 1, b, rows, :]
                pre, pim = probe[0, b, rows, :], probe[1, b, rows, :]
                wave.append((pre * ore - pim * oim, pre * oim + pim * ore))
            for q in range(2):
                for p in range(2):
                    x = wave[0][p] + wave[1][p] if q == 0 else wave[0][p] - wave[1][p]
                    hi, lo = split(x)
                    lhs_hi[q, place, 128 * p : 128 * p + 128] = hi
                    lhs_lo[q, place, 128 * p : 128 * p + 128] = lo

    def correct(k, s, top, low):
        hi, lo = split(top + low if s == 0 else top - low)
        far = left_dot(left[s], hi, lo)
        re, im = far[:128], far[128:]
        factor = amps[k, 128 * s : 128 * s + 128, :].astype(F32) * lax.rsqrt(jnp.maximum(re * re + im * im, 0.25)) - 1.0
        hi, lo = split(jnp.concatenate([re * factor, im * factor], axis=0))
        return left_dot(right[s], hi, lo)

    def deposit(k, u):
        c = lax.rem(corner(positions, k)[1], 128)
        late = lane >= c
        for i in range(0, 256, 64):
            rows = slice(i, i + 64)
            place = slice(256 * u + i, 256 * u + i + 64)
            even, odd = chi[0, place, :], chi[1, place, :]
            g = [[], []]
            for b in range(2):
                x = even + odd if b == 0 else even - odd
                cre, cim = x[:, :128], x[:, 128:]
                pre, pim = probe[0, b, rows, :], probe[1, b, rows, :]
                ore, oim = cut[k, 0, b, rows, :], cut[k, 1, b, rows, :]
                total[b, rows, :] += ore * cre + oim * cim
                total[2 + b, rows, :] += ore * cim - oim * cre
                g[0].append(pltpu.roll(pre * cre + pim * cim, c, 1))
                g[1].append(pltpu.roll(pre * cim - pim * cre, c, 1))
            for p in range(2):
                to = pl.ds(pl.multiple_of(512 * k + 256 + i, 64), 64)
                stage[p, 1, to, :] = jnp.where(late, g[p][0], 0.0)
                stage[p, 2, to, :] = jnp.where(late, g[p][1], g[p][0])
                stage[p, 3, to, :] = jnp.where(late, 0.0, g[p][1])

    def stack(y, u):
        out = []
        for h in range(2):
            rows = slice(256 * u + 128 * h, 256 * u + 128 * h + 128)
            parts = [
                jnp.concatenate([y[0][rows, lanes], y[1][rows, lanes]], axis=1)
                for lanes in (slice(0, 128), slice(128, 256))
            ]
            out.append(jnp.concatenate(parts, axis=0))
        return out

    def visit(j, carry):
        pl.when(j == 1)(functools.partial(heavy.step, 1))
        pl.when(j == pairs - 1)(functools.partial(heavy.step, 2))
        y = [right_dot(lhs_hi[q], lhs_lo[q], right[q]) for q in range(2)]
        for u in range(2):
            deposit(2 * jnp.maximum(j - 1, 0) + u, u)
        half = [[], []]
        for s in range(2):
            for u in range(2):
                top, low = stack(y, u)
                half[u].append(correct(2 * j + u, s, top, low))
        for q in range(2):
            lanes = slice(128 * q, 128 * q + 128)
            parts = []
            for u in range(2):
                for x in (half[u][0] + half[u][1], half[u][0] - half[u][1]):
                    parts.append(jnp.concatenate([x[:128, lanes], x[128:, lanes]], axis=1))
            hi, lo = split(jnp.concatenate(parts, axis=0))
            chi[q] = right_dot(hi, lo, left[q])
        for u in range(2):
            waves(2 * jnp.minimum(j + 1, pairs - 1) + u, u)
        return carry

    for u in range(2):
        waves(u, u)
    lax.fori_loop(0, pairs, visit, jnp.int32(0))
    for u in range(2):
        deposit(2 * pairs - 2 + u, u)


def gather(positions, stage, grad, cols, rows):
    def part(i, carry):
        start = pl.multiple_of(i * 64, 64)
        for p in range(2):
            for b in cols:
                x = jnp.zeros((64, 128), F32)
                for k in range(stage.shape[2] // 512):
                    r, c = corner(positions, k)
                    x = x + stage[p, lax.rem(b + 1 - lax.div(c, 128), 4), pl.ds(512 * k + 256 + start - r, 64), :]
                grad[p, b, pl.ds(start, 64), :] = x
        return carry

    lax.fori_loop(rows.start // 64, rows.stop // 64, part, jnp.int32(0))


def sibling():
    gy, gx = lax.axis_index("gy"), lax.axis_index("gx")
    return gy, gx + 1 - 2 * lax.rem(gx, 2)


def along_x(d):
    gy, gx = lax.axis_index("gy"), lax.axis_index("gx")
    x = lax.div(gx, 4)
    return gy, lax.rem(x + d, 4) * 4 + lax.rem(gx, 4)


def member(j):
    gx = lax.axis_index("gx")
    place = lax.rem(j, 8)
    return lax.div(j, 8) * 4 + lax.div(place, 2), lax.div(gx, 4) * 4 + lax.rem(place, 2) * 2 + lax.rem(gx, 2)


class Sum:
    def __init__(self, total, full, acc0, acc1, acc2, rb0, rb1, rb2, send, recv):
        self.total, self.full, self.acc0, self.acc1, self.acc2 = total, full, acc0, acc1, acc2
        self.rb0, self.rb1, self.rb2 = rb0, rb1, rb2
        self.send, self.recv = send, recv
        gy, gx = lax.axis_index("gy"), lax.axis_index("gx")
        self.core, self.x = lax.rem(gx, 2), lax.div(gx, 4)
        self.mine = lax.rem(gy, 4) * 2 + lax.div(lax.rem(gx, 4), 2)
        self.me = lax.div(gy, 4) * 8 + self.mine
        self.tiles = total.shape[0] // 2

    def greet(self, barrier):
        devices = [sibling()] + [along_x(d) for d in (1, 2, 3)] + [member(lax.rem(self.me + d, 16)) for d in range(1, 16)]
        for device in devices:
            pl.semaphore_signal(barrier, inc=1, device_id=device, device_id_type=MESH)
        return len(devices)

    def copy(self, source, target, i, device):
        return pltpu.make_async_remote_copy(
            source, target, self.send.at[i], self.recv.at[i], device_id=device, device_id_type=MESH
        )

    def copies0(self):
        theirs = pl.ds(pl.multiple_of((1 - self.core) * 128, 128), 128)
        return [self.copy(self.total.at[:, theirs, :], self.rb0, 0, sibling())]

    def copies1(self):
        out = []
        for d in (1, 2, 3):
            part = pl.ds(pl.multiple_of(lax.rem(self.x + d, 4) * 32, 32), 32)
            out.append(self.copy(self.acc0.at[:, part, :], self.rb1.at[d - 1], d, along_x(d)))
        return out

    def copies2(self):
        out = []
        for d in range(1, 16):
            to = lax.rem(self.me + d, 16)
            part = pl.ds(lax.rem(to, 8) * self.tiles, self.tiles)
            out.append(self.copy(self.acc1.at[part], self.rb2.at[self.me], 3 + d, member(to)))
        return out

    def copies3(self):
        place = self.full.at[self.core, self.x, pl.ds(self.mine * self.tiles, self.tiles)]
        out = []
        for d in range(1, 8):
            to = lax.rem(self.mine + d, 8) + lax.div(self.me, 8) * 8
            out.append(self.copy(self.acc2, place, 18 + d, member(to)))
        return out

    def copies4(self):
        place = self.full.at[self.core, self.x]
        return [self.copy(place, place, 25 + d, along_x(d)) for d in (1, 2, 3)]

    def copies5(self):
        place = self.full.at[self.core]
        return [self.copy(place, place, 29, sibling())]

    def step(self, number):
        if number > 0:
            for c in getattr(self, f"copies{number - 1}")():
                c.wait_recv()
        if number == 1:
            own = pl.ds(pl.multiple_of(self.core * 128, 128), 128)
            self.acc0[...] = self.total[:, own, :] + self.rb0[...]
        if number == 2:
            own = pl.ds(pl.multiple_of(self.x * 32, 32), 32)
            x = self.acc0[:, own, :] + self.rb1[0] + self.rb1[1] + self.rb1[2]
            self.acc1[...] = x.reshape(self.acc1.shape)
            self.rb2[pl.ds(self.me, 1)] = self.acc1[pl.ds(self.mine * self.tiles, self.tiles)][None]
        if number == 3:
            x = self.rb2[0]
            for j in range(1, 16):
                x = x + self.rb2[j]
            self.acc2[...] = x
            self.full[pl.ds(self.core, 1), pl.ds(self.x, 1), pl.ds(self.mine * self.tiles, self.tiles)] = x[None, None]
        if number < 6:
            for c in getattr(self, f"copies{number}")():
                c.start()
        else:
            for stage in range(6):
                for c in getattr(self, f"copies{stage}")():
                    c.wait_send()


def sum_scratch(n):
    return [
        pltpu.VMEM((2, 4, 4 * n, 8, 128), F32),
        pltpu.VMEM((n, 128, 128), F32),
        pltpu.VMEM((4 * n, 8, 128), F32),
        pltpu.VMEM((n // 2, 8, 128), F32),
        pltpu.VMEM((n, 128, 128), F32),
        pltpu.VMEM((3, n, 32, 128), F32),
        pltpu.VMEM((16, n // 2, 8, 128), F32),
        pltpu.SemaphoreType.DMA((30,)),
        pltpu.SemaphoreType.DMA((30,)),
    ]


def new_probe(probe, full, weight, write):
    parts = [weight[h, x] for h in range(2) for x in range(4)]
    top = parts[0]
    for w in parts[1:]:
        top = jnp.maximum(top, w)
    floor = 0.1 * jnp.max(top)
    for h in range(2):
        for x in range(4):
            rows = slice(128 * h + 32 * x, 128 * h + 32 * x + 32)
            for b in range(2):
                w = 0.9 * weight[h, x, 4 * b : 4 * b + 4].reshape(32, 128) + floor
                for p in range(2):
                    g = full[h, x, 8 * p + 4 * b : 8 * p + 4 * b + 4].reshape(32, 128)
                    write(p, b, rows, probe[p, b, rows, :] + g / w)


ORDERS = (
    ("s0", "g0", "s1", "g1", "g2", "t3", "go", "s2", "b1", "b2", "t4", "s3", "t5", "s4", "w", "u", "c0", "s5", "c1", "c2", "s6", "t6", "p", "cw"),
    ("s0", "g0", "s1", "g1", "g2", "t3", "go", "s2", "b1", "b2", "t4", "s3", "t5", "s4", "w", "u", "s5", "s6", "t6", "p"),
)


def kernel(positions, obj, probe, amps_far, right_far, left_far, sort_far, obj_out, probe_out, *refs):
    amps, right, left, sort, load, ext, grad, total, acc, probes, arranged, cut, lhs_hi, lhs_lo, chi, stage, inbox, corners, send, recv, *rest = refs
    size = len(rest) // 4
    parts = [rest[size * i : size * (i + 1)] for i in range(4)]
    sums = [Sum(total.at[0:4], *parts[step]) for step in range(2)]
    weights = [Sum(total.at[4:6], *parts[2 + step]) for step in range(2)]
    loads = [
        pltpu.make_async_copy(source, target, load.at[i])
        for i, (source, target) in enumerate(
            ((amps_far.at[0, 0], amps), (sort_far, sort), (right_far, right), (left_far, left))
        )
    ]
    for c in loads:
        c.start()
    for step in range(2):
        blank_outside(ext.at[step])
    barrier, count = greet_sides()
    count = count + sums[0].greet(barrier)
    for b in range(2):
        lanes = slice(128 * b, 128 * b + 128)
        ext[0, :, 1 + b, 128:384, :] = obj[:, :, lanes]
        probes[0, :, b] = probe[:, :, lanes]

    def clear(k, carry):
        for p in range(2):
            for b in range(4):
                stage[p, b, pl.ds(pl.multiple_of(512 * k, 512), 256), :] = jnp.zeros((256, 128), F32)
            stage[p, 0, pl.ds(pl.multiple_of(512 * k + 256, 256), 256), :] = jnp.zeros((256, 128), F32)
        return carry

    lax.fori_loop(0, cut.shape[0], clear, jnp.int32(0))
    stage[:, :, 512 * cut.shape[0] :, :] = jnp.zeros((2, 4, 256, 128), F32)
    pl.semaphore_wait(barrier, count)
    copies = outward(ext.at[0], send.at[0], recv.at[0])
    start_sides(copies["x"] + copies["y"] + copies["i"])
    take_sides(copies["x"])
    start_sides(copies["xy"])
    for c in loads:
        c.wait()
    arrange(amps, sort, arranged)
    take_sides(copies["y"])
    start_sides(copies["iy"])
    take_sides(copies["xy"] + copies["i"] + copies["iy"])
    leave_sides(sum(copies.values(), []))
    for step in range(2):
        old, now = ext.at[step], probes.at[step]
        cut_patches(positions, old, cut, total)
        weights[step].step(0)
        gradients(positions, cut, now, arranged, right, left, total, lhs_hi, lhs_lo, chi, stage, weights[step])
        update(step, positions, stage, grad, inbox.at[step], corners.at[step], acc, old, ext.at[1], now, probes.at[1], sums[step], weights[step], send, recv, obj_out, probe_out)


def update(step, positions, stage, grad, inbox, corners, acc, old, new, now, later, adder, heavy, send, recv, obj_out, probe_out):
    peak = jnp.max(now[0] * now[0] + now[1] * now[1])
    into = inward(grad, inbox, corners, send.at[1 + 2 * step], recv.at[1 + 2 * step])
    out = outward(new, send.at[2], recv.at[2]) if step == 0 else None
    core, up, down, outer = around()
    gx = lax.axis_index("gx")
    inner, halo = pl.ds(2 - core, 1), pl.ds(3 * core, 1)

    def add(where, target, place, value):
        @pl.when(where)
        def _():
            target[place] += value()

    def write(p, b, rows, x):
        if step == 1:
            probe_out[p, rows, 128 * b : 128 * b + 128] = x
        else:
            later[p, b, rows, :] = x

    for event in ORDERS[step]:
        if event in ("g0", "g1"):
            i = int(event[1])
            gather(positions, stage, grad, range(4), (TOP, BOTTOM)[i])
            start_sides([into["xy"][i], into["iy"][i], into["y"][i]])
        elif event == "g2":
            gather(positions, stage, grad, (0, 3), MIDDLE)
            start_sides(into["i"])
        elif event == "go":
            gather(positions, stage, grad, (1, 2), MIDDLE)
            acc[...] = grad[:, 1:3, MIDDLE, :]
        elif event == "b1":
            take_sides(into["iy"])
            add(up, grad, (slice(None), inner, TOP), lambda: corners[:, 2:3])
            add(down, grad, (slice(None), inner, BOTTOM), lambda: corners[:, 3:4])
            start_sides(into["z"])
        elif event == "b2":
            take_sides(into["xy"])
            add(down & outer, grad, (slice(None), halo, LOWER), lambda: corners[:, 0:1])
            add(up & outer, grad, (slice(None), halo, UPPER), lambda: corners[:, 1:2])
            start_sides(into["x"])
        elif event == "w":
            take_sides(into["y"] + into["z"] + into["i"] + into["x"])
            leave_sides(sum(into.values(), []))
            every = slice(None)
            add(down, acc, (every, every, slice(128, 256)), lambda: inbox[:, 1:3, TOP])
            add(up, acc, (every, every, slice(0, 128)), lambda: inbox[:, 1:3, BOTTOM])
            add(gx > 0, acc, (every, 0), lambda: inbox[:, 3, MIDDLE])
            add(gx < lax.axis_size("gx") - 1, acc, (every, 1), lambda: inbox[:, 0, MIDDLE])
        elif event == "c0":
            start_sides(out["x"] + out["y"] + out["i"])
        elif event == "c1":
            take_sides(out["x"])
            start_sides(out["xy"])
        elif event == "c2":
            take_sides(out["y"])
            start_sides(out["iy"])
        elif event == "cw":
            take_sides(out["xy"] + out["i"] + out["iy"])
            leave_sides(sum(out.values(), []))
        elif event[0] == "s":
            adder.step(int(event[1]))
        elif event[0] == "t":
            heavy.step(int(event[1]))
        elif event == "u" and step == 1:
            for b in range(2):
                obj_out[:, :, 128 * b : 128 * b + 128] = old[:, 1 + b, 128:384, :] + acc[:, b] / peak
        elif event == "u":
            new[:, 1:3, 128:384, :] = old[:, 1:3, 128:384, :] + acc[...] / peak
        else:
            new_probe(now, adder.full, heavy.full, write)


def shards(obj, probe, positions, amps):
    count = positions.shape[2]
    right, left = (jnp.asarray(t) for t in tables())
    tile = jax.ShapeDtypeStruct((2, 256, 256), F32)
    ext = (2, 4, 512, 128)
    anywhere = pl.BlockSpec(memory_space=pl.ANY)
    return pl.pallas_call(
        kernel,
        out_shape=(tile, tile),
        in_specs=[SMEM] + [VMEM] * 2 + [anywhere] * 4,
        out_specs=(VMEM, VMEM),
        scratch_shapes=[
            pltpu.VMEM((count, 256, 256), BF16),
            pltpu.VMEM((2, 2, 256, 256), BF16),
            pltpu.VMEM((2, 2, 256, 256), BF16),
            pltpu.VMEM((2, 256, 256), BF16),
            pltpu.SemaphoreType.DMA((4,)),
            pltpu.VMEM((2, *ext), F32),
            pltpu.VMEM(ext, F32),
            pltpu.VMEM((6, 256, 128), F32),
            pltpu.VMEM((2, 2, 256, 128), F32),
            pltpu.VMEM((2, 2, 2, 256, 128), F32),
            pltpu.VMEM((count, 256, 256), BF16),
            pltpu.VMEM((count, 2, 2, 256, 128), F32),
            pltpu.VMEM((2, 512, 256), BF16),
            pltpu.VMEM((2, 512, 256), BF16),
            pltpu.VMEM((2, 512, 256), F32),
            pltpu.VMEM((2, 4, 512 * count + 256, 128), F32),
            pltpu.VMEM((2, *ext), F32),
            pltpu.VMEM((2, 2, 4, 128, 128), F32),
            pltpu.SemaphoreType.DMA((4, 16)),
            pltpu.SemaphoreType.DMA((4, 16)),
            *sum_scratch(4) * 2,
            *sum_scratch(2) * 2,
        ],
        compiler_params=pltpu.CompilerParams(collective_id=0, has_side_effects=True, vmem_limit_bytes=VMEM_LIMIT),
        name="iterations",
    )(jnp.swapaxes(positions, 2, 3), obj, probe, amps, right, left, jnp.asarray(sorting()))


def solution(mesh):
    in_specs = (
        P(None, "gy", "gx"),
        P(),
        P("gy", "gx", None, None),
        P("gy", "gx", None, None, None),
    )
    out_specs = (P(None, "gy", "gx"), P())
    return jax.shard_map(shards, mesh=mesh, in_specs=in_specs, out_specs=out_specs, check_vma=False)
```
